256 devices in a mesh: seq: 32 (over y, z), head: 8 (over x, core).
Axes of the slice: x: 4, y: 4, z: 8, core: 2. Of those that a mesh axis runs over, the one named last changes fastest.
Arguments:
- query_nope: bfloat16 [4096, 16384], P(('seq', 'head')), may hold values from -6 to 6
- query_rope: bfloat16 [4096, 8192], P(('seq', 'head')), may hold values from -60 to 60
- absorb_key: bfloat16 [128, 128, 512], P('head'), may hold values from -0.5 to 0.5
- value_absorption_matrix: bfloat16 [128, 512, 128], P('head'), may hold values from -3 to 3
- prompt_latent: bfloat16 [512, 24576], P(None, 'seq'), may hold values from -6 to 6
- prompt_rope: bfloat16 [64, 24576], P(None, 'seq'), may hold values from -6 to 6
- response_latent: bfloat16 [512, 4096], P(None, 'seq'), may hold values from -6 to 6
- response_rope: bfloat16 [64, 4096], P(None, 'seq'), may hold values from -2.5 to 2.5
- prompt_lengths: int32 [16], replicated, may hold values from 768 to 2304, as said below
- prompt_of: int32 [4096], P('seq'), may hold values from 0 to 15, as said below
- response_start: int32 [4096], P('seq'), may hold values from 0 to 4095, as said below
Outputs:
- attended: bfloat16 [4096, 16384], P(('seq', 'head'))
The draws below stay inside these ranges and needn't reach their ends.
Inputs may be any that keep to these rules, and one draw needn't show every extreme that they name: `prompt_lengths`: the lengths sum to 24576; the longest is exactly 2304. `prompt_of`: constant over each response. The prompt of token t owns at least one of the cache columns t // 128 * 768 to (t // 128 + 1) * 768 - 1. response_start[t] <= t, and response_start[t] lies in the same aligned block of 128 tokens as t; either response_start[t] == t or response_start[t] == response_start[t - 1].
All inputs are finite; a program needn't handle non-finite values.
Results may differ from the reference program's by a relative error of at most 0.008.
Values may be sent and summed in bfloat16 or wider, within the bound.
No kernel may reach another device: no remote copies, remote signals or barrier semaphores. Data moves between devices by JAX's collectives and lax.ppermute only.
A program may use at most 64 MiB of HBM per device.

```python
import jax
import jax.numpy as jnp
from jax import lax

H = 128
KV = 512
ROPE = 64
NOPE = 128
VD = 128
P_DEV = 768
R_DEV = 128
PMAX = 2304
NP = 16
P_TOK = 24576
R_TOK = 4096


def layout(key):
    key_lengths, key_order, key_flags, key_choice, key_marks, key_signs = jax.random.split(key, 6)
    pair_count = (NP - 3) // 2
    spread = jax.random.randint(key_lengths, (pair_count,), -P_DEV, P_DEV + 1).astype(jnp.int32)
    pieces = [jnp.array([PMAX, 3 * P_DEV // 2, 3 * P_DEV // 2], jnp.int32), 2 * P_DEV + spread, 2 * P_DEV - spread]
    if (NP - 3) % 2 == 1:
        pieces.append(jnp.array([2 * P_DEV], jnp.int32))
    lengths = jnp.concatenate(pieces)[jax.random.permutation(key_order, NP)]
    prompt_ends = jnp.cumsum(lengths, dtype=jnp.int32)
    prompt_starts = prompt_ends - lengths
    block_count = R_TOK // R_DEV
    block_low = jnp.arange(block_count, dtype=jnp.int32) * P_DEV
    first_prompt = jnp.sum((prompt_ends[None, :] <= block_low[:, None]).astype(jnp.int32), axis=1)
    last_prompt = jnp.sum((prompt_starts[None, :] < block_low[:, None] + P_DEV).astype(jnp.int32), axis=1) - 1
    positions = jnp.arange(R_TOK, dtype=jnp.int32)
    within = positions % R_DEV
    owner_block = positions // R_DEV
    start_flags = (jax.random.randint(key_flags, (R_TOK,), 0, R_DEV // 2) == 0) | (within == 0)
    response_first = lax.cummax(jnp.where(start_flags, positions, 0), axis=0)
    raw_pick = jax.random.randint(key_choice, (R_TOK,), 0, 1 << 20)[response_first]
    choice_count = last_prompt - first_prompt + 1
    prompt_ids = (first_prompt[owner_block] + raw_pick % choice_count[owner_block]).astype(jnp.int32)
    marked = (jax.random.randint(key_marks, (R_TOK,), 0, 8) == 0) & ((positions - response_first) % 2 == 1)
    partner = jnp.concatenate([marked[1:], jnp.zeros((1,), jnp.bool_)])
    sign_table = (jax.random.randint(key_signs, (R_TOK, ROPE), 0, 2) * 2 - 1).astype(jnp.float32)
    sign_next = jnp.concatenate([sign_table[1:], sign_table[:1]], axis=0)
    return (lengths, prompt_ids, response_first, marked, partner, sign_table, sign_next)


def draw_prompt_lengths(key, part):
    shared = layout(key)
    return shared[0].astype(jnp.int32)


def draw_prompt_of(key, part):
    shared = layout(key)
    return shared[1].astype(jnp.int32)


def draw_response_start(key, part):
    shared = layout(key)
    return shared[2].astype(jnp.int32)


def draw_query_rope(key, part):
    key = jax.random.fold_in(key, 11)
    values = jnp.clip(jax.random.normal(key, (R_TOK, H, ROPE), jnp.float32), -4.0, 4.0)
    return values.reshape(R_TOK, H * ROPE).astype(jnp.bfloat16)


def draw_response_rope(key, part):
    key = jax.random.fold_in(key, 13)
    values = jnp.clip(jax.random.normal(key, (R_TOK, ROPE), jnp.float32), -2.5, 2.5)
    return values.T.astype(jnp.bfloat16)


def level_of(key, shape, shards, low, top_value):
    factor_of = 1.0
    for axis_at, shards_of in shards:
        steps = jax.random.uniform(jax.random.fold_in(jax.random.fold_in(key, 6), axis_at), (shards_of,), jnp.float32, low / len(shards), top_value / len(shards))
        factor_of = factor_of * jnp.repeat(jnp.exp(steps), shape[axis_at] // shards_of).reshape((-1,) + (1,) * (len(shape) - 1 - axis_at))
    return factor_of


def centred(own_key, shape, scale, reach, cuts=(), held_as=jnp.bfloat16):
    result = scale * jax.random.normal(own_key, shape, jnp.float32)
    if cuts:
        result = result * level_of(own_key, shape, cuts, -0.22, 0.18)
    return jnp.clip(result, -reach, reach).astype(held_as)


def setup_inputs(seed: int = 0) -> dict:
    keys = jax.random.split(jax.random.key(seed), 12)
    return {
        "query_nope": centred(keys[0], (R_TOK, H * NOPE), 1.0, 6.0, ((0, 256),)),
        "query_rope": draw_query_rope(jax.random.fold_in(keys[11], 71), 0),
        "absorb_key": centred(keys[2], (H, NOPE, KV), NOPE ** -0.5, 0.5, ((0, 8),)),
        "value_absorption_matrix": centred(keys[3], (H, KV, VD), 0.5, 3.0, ((0, 8),)),
        "prompt_latent": centred(keys[4], (KV, P_TOK), 1.0, 6.0, ((1, 32),)),
        "prompt_rope": centred(keys[5], (ROPE, P_TOK), 1.0, 6.0, ((1, 32),)),
        "response_latent": centred(keys[6], (KV, R_TOK), 1.0, 6.0, ((1, 32),)),
        "response_rope": draw_response_rope(jax.random.fold_in(keys[11], 71), 0),
        "prompt_lengths": draw_prompt_lengths(jax.random.fold_in(keys[11], 71), 0),
        "prompt_of": draw_prompt_of(jax.random.fold_in(keys[11], 71), 0),
        "response_start": draw_response_start(jax.random.fold_in(keys[11], 71), 0),
    }


def rounded(values):
    return lax.optimization_barrier(values.astype(jnp.bfloat16)).astype(jnp.float32)


def reference(query_nope, query_rope, absorb_key, value_absorption_matrix, prompt_latent, prompt_rope, response_latent, response_rope, prompt_lengths, prompt_of, response_start):
    block_count = R_TOK // R_DEV
    reach_blocks = PMAX // P_DEV
    window = min(2 * reach_blocks + 1, block_count) * P_DEV
    prompt_ends = jnp.cumsum(prompt_lengths, dtype=jnp.int32)
    prompt_starts = prompt_ends - prompt_lengths
    score_scale = (NOPE + ROPE) ** -0.5
    key_float = absorb_key.astype(jnp.float32)
    value_single_precision = value_absorption_matrix.astype(jnp.float32)

    def one_block(block_index):
        first_token = (block_index * R_DEV).astype(jnp.int32)
        unrotated_row_values = lax.dynamic_slice_in_dim(query_nope, first_token, R_DEV, 0).astype(jnp.float32).reshape(R_DEV, H, NOPE)
        rope_rows = lax.dynamic_slice_in_dim(query_rope, first_token, R_DEV, 0).astype(jnp.float32).reshape(R_DEV, H, ROPE)
        query_latent = rounded(jnp.einsum("thn,hnk->htk", unrotated_row_values, key_float))
        first_column = jnp.clip((block_index - reach_blocks) * P_DEV, 0, block_count * P_DEV - window).astype(jnp.int32)
        cache_latent = lax.dynamic_slice_in_dim(prompt_latent, first_column, window, 1)
        cache_rope = lax.dynamic_slice_in_dim(prompt_rope, first_column, window, 1)
        own_latent = lax.dynamic_slice_in_dim(response_latent, first_token, R_DEV, 1)
        own_rope = lax.dynamic_slice_in_dim(response_rope, first_token, R_DEV, 1)
        all_latent = jnp.concatenate([cache_latent, own_latent], axis=1).astype(jnp.float32)
        all_rope = jnp.concatenate([cache_rope, own_rope], axis=1).astype(jnp.float32)
        owners = lax.dynamic_slice_in_dim(prompt_of, first_token, R_DEV, 0)
        range_low = prompt_starts[owners]
        range_high = prompt_ends[owners]
        columns = first_column + jnp.arange(window, dtype=jnp.int32)
        inside_prompt_flags = (columns[None, :] >= range_low[:, None]) & (columns[None, :] < range_high[:, None])
        token_pos = first_token + jnp.arange(R_DEV, dtype=jnp.int32)
        starts = lax.dynamic_slice_in_dim(response_start, first_token, R_DEV, 0)
        causal = (token_pos[None, :] >= starts[:, None]) & (token_pos[None, :] <= token_pos[:, None])
        allowed = jnp.concatenate([inside_prompt_flags, causal], axis=1)
        scores = jnp.einsum("htk,kj->htj", query_latent, all_latent) + jnp.einsum("thr,rj->htj", rope_rows, all_rope)
        scores = jnp.where(allowed[None], scores * score_scale, -jnp.inf)
        row_max = jnp.max(scores, axis=2, keepdims=True)
        weights = jnp.exp(scores - row_max)
        totals = jnp.sum(weights, axis=2, keepdims=True)
        latent_output = rounded(jnp.einsum("htj,kj->htk", rounded(weights), all_latent) / totals)
        attended = jnp.einsum("qwz,qzf->wqf", latent_output, value_single_precision)
        return attended.astype(jnp.bfloat16).reshape(R_DEV, H * VD)

    blocks = lax.map(one_block, jnp.arange(block_count, dtype=jnp.int32))
    return blocks.reshape(R_TOK, H * VD)
```

```python
import math

import jax
import jax.numpy as jnp
from jax import lax
from jax.experimental import pallas as pl
from jax.experimental.pallas import tpu as pltpu
from jax.sharding import PartitionSpec as P

PMAX = 2304
TILE = 16
LANES = 128
CHUNK = 256
NEG = -1e30
MIB = 1024 * 1024


def absorb_kernel(queries_ref, absorb_ref, out_ref):
    head_count, nope, latent = absorb_ref.shape
    tokens = queries_ref.shape[0]
    tiles = tokens // TILE
    rope = out_ref.shape[3] - latent
    for h in range(head_count):
        part = jnp.dot(
            queries_ref[:, h * nope : (h + 1) * nope],
            absorb_ref[h],
            preferred_element_type=jnp.float32,
        ).astype(jnp.bfloat16)
        out_ref[:, h, :, :latent] = part.reshape(tiles, TILE, latent)
        first = head_count * nope + h * rope
        out_ref[:, h, :, latent:] = queries_ref[:, first : first + rope].reshape(tiles, TILE, rope)


def attend_kernel(
    score_scale,
    position_ref,
    lengths_ref,
    prompt_of_ref,
    response_start_ref,
    queries_ref,
    response_ref,
    value_ref,
    own_ref,
    mine1_ref,
    mine2_ref,
    mine3_ref,
    theirs1_ref,
    theirs2_ref,
    theirs3_ref,
    out_ref,
    window,
    scores,
    accumulated,
    latent_out,
    sems,
):
    block = own_ref.shape[1]
    reach = PMAX // block
    tiles, rows, width = queries_ref.shape
    head_count, latent, value_width = value_ref.shape
    span = window.shape[1]
    seq_index = position_ref[0]
    core = position_ref[1]

    copies = [pltpu.make_async_copy(own_ref, window.at[:, pl.ds(reach * block, block)], sems.at[0])]
    for r, (mine, theirs) in enumerate(
        ((mine1_ref, theirs1_ref), (mine2_ref, theirs2_ref), (mine3_ref, theirs3_ref)), 1
    ):
        down = pl.multiple_of((reach - r + 2 * r * core) * block, LANES)
        up = pl.multiple_of((reach + r - 2 * r * core) * block, LANES)
        copies.append(
            pltpu.make_async_copy(mine, window.at[:, pl.ds(down, block)], sems.at[2 * r - 1])
        )
        copies.append(
            pltpu.make_async_copy(theirs, window.at[:, pl.ds(up, block)], sems.at[2 * r])
        )
    for copy in copies:
        copy.start()

    token_count = tiles * TILE
    first_column = (seq_index - reach) * block
    first_token = seq_index * token_count
    prompt_of = prompt_of_ref[...]
    low = jnp.zeros_like(prompt_of)
    high = jnp.zeros_like(prompt_of)
    start = -first_column
    for p in range(lengths_ref.shape[0]):
        chosen = prompt_of == p
        end = start + lengths_ref[p]
        low = jnp.where(chosen, start, low)
        high = jnp.where(chosen, end, high)
        start = end
    response_start = response_start_ref[...] - first_token
    factor = score_scale * math.log2(math.e)
    lane = lax.broadcasted_iota(jnp.int32, (TILE, LANES), 1)
    sub = lax.broadcasted_iota(jnp.int32, (TILE, LANES), 0)

    for copy in copies:
        copy.wait()

    for tile in range(tiles):
        own = slice(tile * TILE, (tile + 1) * TILE)
        tile_low, tile_high = low[own], high[own]
        least = jnp.min(tile_low[:, :1])
        most = jnp.max(tile_high[:, :1])
        base = least // LANES * LANES
        count = (most - base + CHUNK - 1) // CHUNK
        base = jnp.minimum(base, span - count * CHUNK)
        queries = queries_ref[tile]

        def masked(values, allowed):
            columns = values.shape[1]
            shaped = values.reshape(head_count, TILE, columns)
            return jnp.where(allowed[None], shaped, NEG).reshape(rows, columns)

        causal = (lane >= response_start[own]) & (lane <= sub + tile * TILE)
        own_scores = masked(
            jnp.dot(queries, response_ref[...], preferred_element_type=jnp.float32), causal
        )

        def score(i, largest):
            at = pl.multiple_of(base + i * CHUNK, LANES)
            values = jnp.dot(
                queries, window[:, pl.ds(at, CHUNK)], preferred_element_type=jnp.float32
            )
            for j in range(CHUNK // LANES):
                column = lane + (at + j * LANES)
                allowed = (column >= tile_low) & (column < tile_high)
                part = masked(values[:, j * LANES : (j + 1) * LANES], allowed)
                scores[i, :, j * LANES : (j + 1) * LANES] = part
                largest = jnp.maximum(largest, part)
            return largest

        largest = lax.fori_loop(0, count, score, own_scores)
        largest = jnp.max(largest, axis=1, keepdims=True) * factor
        weights = jnp.exp2(own_scores * factor - largest)
        accumulated[...] = lax.dot_general(
            weights.astype(jnp.bfloat16),
            response_ref[:latent, :],
            (((1,), (1,)), ((), ())),
            preferred_element_type=jnp.float32,
        )

        def weigh(i, totals):
            at = pl.multiple_of(base + i * CHUNK, LANES)
            weights = jnp.exp2(scores[i] * factor - largest)
            accumulated[...] += lax.dot_general(
                weights.astype(jnp.bfloat16),
                window[:latent, pl.ds(at, CHUNK)],
                (((1,), (1,)), ((), ())),
                preferred_element_type=jnp.float32,
            )
            for j in range(CHUNK // LANES):
                totals = totals + weights[:, j * LANES : (j + 1) * LANES]
            return totals

        totals = lax.fori_loop(0, count, weigh, weights)
        totals = jnp.sum(totals, axis=1, keepdims=True)
        latent_out[:, own, :] = (
            (accumulated[...] / totals).astype(jnp.bfloat16).reshape(head_count, TILE, latent)
        )

    for h in range(head_count):
        attended = jnp.dot(latent_out[h], value_ref[h], preferred_element_type=jnp.float32)
        out_ref[:, :, h * value_width : (h + 1) * value_width] = attended.astype(
            jnp.bfloat16
        ).reshape(tiles, TILE, value_width)


def absorb(queries, absorb_key, rope):
    head_count, nope, latent = absorb_key.shape
    tokens = queries.shape[0]
    return pl.pallas_call(
        absorb_kernel,
        out_shape=jax.ShapeDtypeStruct(
            (tokens // TILE, head_count, TILE, latent + rope), jnp.bfloat16
        ),
        name="absorb",
        cost_estimate=pl.CostEstimate(
            flops=2 * tokens * head_count * nope * latent,
            bytes_accessed=6 * MIB,
            transcendentals=0,
        ),
        compiler_params=pltpu.CompilerParams(vmem_limit_bytes=24 * MIB),
    )(queries, absorb_key)


def attend(position, lengths, prompt_of, response_start, queries, response, value, own, mine, theirs):
    head_count, latent, value_width = value.shape
    tiles, rows, width = queries.shape
    block = own.shape[1]
    span = (2 * (PMAX // block) + 1) * block
    longest = 2 * PMAX + LANES
    vmem = pl.BlockSpec(memory_space=pltpu.VMEM)
    smem = pl.BlockSpec(memory_space=pltpu.SMEM)
    anywhere = pl.BlockSpec(memory_space=pl.ANY)
    score_scale = (192) ** (-0.5)
    return pl.pallas_call(
        lambda *refs: attend_kernel(score_scale, *refs),
        out_shape=jax.ShapeDtypeStruct((tiles, TILE, head_count * value_width), jnp.bfloat16),
        in_specs=[smem, smem] + [vmem] * 5 + [anywhere] * 7,
        out_specs=vmem,
        scratch_shapes=[
            pltpu.VMEM((width, span), jnp.bfloat16),
            pltpu.VMEM((-(-longest // CHUNK), rows, CHUNK), jnp.float32),
            pltpu.VMEM((rows, latent), jnp.float32),
            pltpu.VMEM((head_count, tiles * TILE, latent), jnp.bfloat16),
            pltpu.SemaphoreType.DMA((7,)),
        ],
        name="attend",
        cost_estimate=pl.CostEstimate(
            flops=2 * tiles * rows * (width + latent) * 2432,
            bytes_accessed=12 * MIB,
            transcendentals=tiles * rows * 2432,
        ),
        compiler_params=pltpu.CompilerParams(vmem_limit_bytes=48 * MIB),
    )(position, lengths, prompt_of, response_start, queries, response, value, own, *mine, *theirs)


def local(
    query_nope,
    query_rope,
    absorb_key,
    value_absorption_matrix,
    prompt_latent,
    prompt_rope,
    response_latent,
    response_rope,
    prompt_lengths,
    prompt_of,
    response_start,
):
    head_count, nope_width, latent_width = absorb_key.shape
    value_width = value_absorption_matrix.shape[2]
    rope_width = prompt_rope.shape[0]
    block = prompt_latent.shape[1]
    tokens = response_latent.shape[1]
    groups = lax.axis_size("head")
    length = lax.axis_size("seq")
    seq_index = lax.axis_index("seq")
    head_index = lax.axis_index("head")

    own = jnp.concatenate([prompt_latent, prompt_rope], axis=0)
    onward = [
        (i * groups + h, (i + by) * groups + h)
        for i in range(length)
        for h in range(groups)
        for by in (1 - 2 * (h % 2),)
        if 0 <= i + by < length
    ]
    swapped = [(h, h ^ 1) for h in range(groups)]
    mine, theirs = [], []
    held = own
    for _ in range(PMAX // block):
        held = lax.ppermute(held, ("seq", "head"), onward)
        mine.append(held)
        theirs.append(lax.ppermute(held, "head", swapped))

    per = tokens // groups
    sent = jnp.concatenate(
        [
            query_nope.reshape(per, groups, head_count * nope_width),
            query_rope.reshape(per, groups, head_count * rope_width),
        ],
        axis=2,
    ).transpose(1, 0, 2)
    arrived = lax.all_to_all(sent, "head", split_axis=0, concat_axis=0, tiled=True)
    queries = absorb(
        arrived.reshape(tokens, head_count * (nope_width + rope_width)), absorb_key, rope_width
    )
    response = jnp.concatenate([response_latent, response_rope], axis=0)
    position = jnp.stack([seq_index, head_index % 2]).astype(jnp.int32)
    attended = attend(
        position,
        prompt_lengths,
        jnp.broadcast_to(prompt_of[:, None], (tokens, LANES)),
        jnp.broadcast_to(response_start[:, None], (tokens, LANES)),
        queries.reshape(tokens // TILE, head_count * TILE, latent_width + rope_width),
        response,
        value_absorption_matrix,
        own,
        mine,
        theirs,
    )
    returned = lax.all_to_all(attended, "head", split_axis=0, concat_axis=0, tiled=True)
    return returned.transpose(1, 0, 2).reshape(per, groups * head_count * value_width)


def solution(mesh):
    return jax.shard_map(
        local,
        mesh=mesh,
        in_specs=(
            P(("seq", "head"), None),
            P(("seq", "head"), None),
            P("head", None, None),
            P("head", None, None),
            P(None, "seq"),
            P(None, "seq"),
            P(None, "seq"),
            P(None, "seq"),
            P(),
            P("seq"),
            P("seq"),
        ),
        out_specs=P(("seq", "head"), None),
        check_vma=False,
    )
```

```python
import math

import jax
import jax.numpy as jnp
from jax import lax
from jax.experimental import pallas as pl
from jax.experimental.pallas import tpu as pltpu
from jax.sharding import PartitionSpec as P

PMAX = 2304
REACH = 3
GROUP = 16
TILE = 32
LANES = 128
NEAR_CHUNK = 512
FAR_CHUNK = 384
NEG = -1e30
MIB = 1024 * 1024

VMEM = pl.BlockSpec(memory_space=pltpu.VMEM)
SMEM = pl.BlockSpec(memory_space=pltpu.SMEM)
ANYWHERE = pl.BlockSpec(memory_space=pl.ANY)


def pack_kernel(
    nope_ref,
    rope_ref,
    latent_ref,
    key_rope_ref,
    response_latent_ref,
    response_rope_ref,
    own_ref,
    sent_ref,
    response_ref,
    sems,
):
    latent = latent_ref.shape[0]
    groups, _, width = sent_ref.shape
    nope = nope_ref.shape[1] // groups
    rope = rope_ref.shape[1] // groups
    pairs = [
        (latent_ref, own_ref.at[:latent]),
        (key_rope_ref, own_ref.at[latent:]),
        (response_latent_ref, response_ref.at[:latent]),
        (response_rope_ref, response_ref.at[latent:]),
    ]
    for g in range(groups):
        pairs.append((nope_ref.at[:, g * nope : (g + 1) * nope], sent_ref.at[g, :, :nope]))
        pairs.append((rope_ref.at[:, g * rope : (g + 1) * rope], sent_ref.at[g, :, nope:]))
    copies = [
        pltpu.make_async_copy(source, target, sems.at[i])
        for i, (source, target) in enumerate(pairs)
    ]
    for copy in copies:
        copy.start()
    for copy in copies:
        copy.wait()


def absorb_kernel(
    position_ref,
    lengths_ref,
    prompt_of_ref,
    queries_ref,
    absorb_ref,
    out_ref,
    low_ref,
    high_ref,
    bounds_ref,
):
    head_count, nope, latent = absorb_ref.shape
    tokens = queries_ref.shape[0]
    tiles = tokens // TILE
    rope = out_ref.shape[3] - latent
    for h in range(head_count):
        part = jnp.dot(
            queries_ref[:, h * nope : (h + 1) * nope],
            absorb_ref[h],
            preferred_element_type=jnp.float32,
        ).astype(jnp.bfloat16)
        out_ref[:, h, :, :latent] = part.reshape(tiles, TILE, latent)
        first = head_count * nope + h * rope
        out_ref[:, h, :, latent:] = queries_ref[:, first : first + rope].reshape(tiles, TILE, rope)
    prompt_of = prompt_of_ref[...]
    low = jnp.zeros_like(prompt_of)
    high = jnp.zeros_like(prompt_of)
    start = -position_ref[2]
    for p in range(lengths_ref.shape[0]):
        chosen = prompt_of == p
        end = start + lengths_ref[p]
        low = jnp.where(chosen, start, low)
        high = jnp.where(chosen, end, high)
        start = end
    low_ref[...] = low
    high_ref[...] = high
    for tile in range(tiles):
        own = slice(tile * TILE, (tile + 1) * TILE)
        bounds_ref[2 * tile] = jnp.min(low[own, :1])
        bounds_ref[2 * tile + 1] = jnp.max(high[own, :1])


def place(least, most, chunk, span):
    base = least // LANES * LANES
    count = (most - base + chunk - 1) // chunk
    return jnp.minimum(base, span - count * chunk), count


def masked(part, factor, allowed):
    rows, columns = part.shape
    shaped = (part * factor).reshape(rows // TILE, TILE, columns)
    return jnp.where(allowed[None], shaped, NEG).reshape(rows, columns)


def loop(first, last, body):
    @pl.loop(first, last)
    def _(i):
        body(i)


def score_chunk(queries, window, at, chunk, factor, low, high, lane, scores, slot, peak):
    values = jnp.dot(queries, window[:, pl.ds(at, chunk)], preferred_element_type=jnp.float32)
    largest = peak[...]
    for j in range(chunk // LANES):
        column = lane + (at + j * LANES)
        part = values[:, j * LANES : (j + 1) * LANES]
        part = masked(part, factor, (column >= low) & (column < high))
        scores[slot, :, j * LANES : (j + 1) * LANES] = part
        largest = jnp.maximum(largest, part)
    peak[...] = largest


def weigh_chunk(scores, slot, window, at, chunk, latent, peak, sums, total):
    peak = peak[...]
    parts = [
        jnp.exp2(scores[slot, :, j * LANES : (j + 1) * LANES] - peak) for j in range(chunk // LANES)
    ]
    weights = jnp.concatenate([part.astype(jnp.bfloat16) for part in parts], axis=1)
    total[...] += lax.dot_general(
        weights,
        window[:latent, pl.ds(at, chunk)],
        (((1,), (1,)), ((), ())),
        preferred_element_type=jnp.float32,
    )
    added = parts[0]
    for part in parts[1:]:
        added = added + part
    sums[...] += added


def spread_peak(peak):
    peak[...] = jnp.broadcast_to(jnp.max(peak[...], axis=1, keepdims=True), peak.shape)


def near_kernel(
    factor,
    position_ref,
    bounds_ref,
    low_ref,
    high_ref,
    response_start_ref,
    queries_ref,
    response_ref,
    own_ref,
    mine1_ref,
    theirs1_ref,
    mine2_ref,
    theirs2_ref,
    total_ref,
    peak_ref,
    sums_ref,
    window,
    scores_even,
    scores_odd,
    sems,
):
    block = own_ref.shape[1]
    tiles, rows, _ = queries_ref.shape
    latent = total_ref.shape[2]
    span = window.shape[1]
    core = position_ref[1]
    copies = [
        pltpu.make_async_copy(own_ref, window.at[:, pl.ds(2 * block, block)], sems.at[0])
    ]
    for r, (mine, theirs) in enumerate(((mine1_ref, theirs1_ref), (mine2_ref, theirs2_ref)), 1):
        down = pl.multiple_of((2 - r + 2 * r * core) * block, LANES)
        up = pl.multiple_of((2 + r - 2 * r * core) * block, LANES)
        copies.append(
            pltpu.make_async_copy(mine, window.at[:, pl.ds(down, block)], sems.at[2 * r - 1])
        )
        copies.append(
            pltpu.make_async_copy(theirs, window.at[:, pl.ds(up, block)], sems.at[2 * r])
        )
    for copy in copies:
        copy.start()
    filled = (2 * REACH - 1) * block
    window[:, filled:] = jnp.zeros((window.shape[0], span - filled), window.dtype)

    lane = lax.broadcasted_iota(jnp.int32, (TILE, LANES), 1)
    sub = lax.broadcasted_iota(jnp.int32, (TILE, LANES), 0)
    response_start = response_start_ref[...] - position_ref[0]
    all_rows = queries_ref[...].reshape(tiles * rows, queries_ref.shape[2])
    own_scores = jnp.dot(all_rows, response_ref[...], preferred_element_type=jnp.float32)
    for tile in range(tiles):
        own = slice(tile * TILE, (tile + 1) * TILE)
        causal = (lane >= response_start[own]) & (lane <= sub + tile * TILE)
        part = masked(own_scores[tile * rows : (tile + 1) * rows], factor, causal)
        sums_ref[tile] = part
        peak_ref[tile] = part

    def bound(i):
        return jnp.clip(bounds_ref[i] - block, 0, filled)

    places = [
        place(bound(2 * tile), bound(2 * tile + 1), NEAR_CHUNK, span) for tile in range(tiles)
    ]
    scores = (scores_even, scores_odd)

    def score(tile, i):
        own = slice(tile * TILE, (tile + 1) * TILE)
        at = pl.multiple_of(places[tile][0] + i * NEAR_CHUNK, LANES)
        score_chunk(
            queries_ref[tile],
            window,
            at,
            NEAR_CHUNK,
            factor,
            low_ref[own] - block,
            jnp.minimum(high_ref[own] - block, filled),
            lane,
            scores[tile % 2],
            i,
            peak_ref.at[tile],
        )

    def weigh(tile, i):
        at = pl.multiple_of(places[tile][0] + i * NEAR_CHUNK, LANES)
        weigh_chunk(
            scores[tile % 2],
            i,
            window,
            at,
            NEAR_CHUNK,
            latent,
            peak_ref.at[tile],
            sums_ref.at[tile],
            total_ref.at[tile],
        )

    for copy in copies:
        copy.wait()
    loop(0, places[0][1], lambda i: score(0, i))
    for tile in range(tiles):
        spread_peak(peak_ref.at[tile])
        weights = jnp.exp2(sums_ref[tile] - peak_ref[tile])
        sums_ref[tile] = weights
        total_ref[tile] = lax.dot_general(
            weights.astype(jnp.bfloat16),
            response_ref[:latent, :],
            (((1,), (1,)), ((), ())),
            preferred_element_type=jnp.float32,
        )
        count = places[tile][1]
        if tile + 1 < tiles:
            following = places[tile + 1][1]
            both = jnp.minimum(count, following)

            def fused(i):
                weigh(tile, i)
                score(tile + 1, i)

            loop(0, both, fused)
            loop(both, following, lambda i: score(tile + 1, i))
            loop(both, count, lambda i: weigh(tile, i))
        else:
            loop(0, count, lambda i: weigh(tile, i))


def far_kernel(
    factor,
    position_ref,
    bounds_ref,
    low_ref,
    high_ref,
    queries_ref,
    total_in_ref,
    peak_in_ref,
    sums_in_ref,
    value_ref,
    mine_ref,
    theirs_ref,
    out_ref,
    window,
    scores,
    total,
    peak,
    sums,
    latent_out,
    sems,
):
    block = mine_ref.shape[1]
    tiles, rows, _ = queries_ref.shape
    head_count, latent, value_width = value_ref.shape
    span = window.shape[1]
    core = position_ref[1]
    mine_at = pl.multiple_of(core * block, LANES)
    theirs_at = pl.multiple_of((1 - core) * block, LANES)
    copies = [
        pltpu.make_async_copy(mine_ref, window.at[:, pl.ds(mine_at, block)], sems.at[0]),
        pltpu.make_async_copy(theirs_ref, window.at[:, pl.ds(theirs_at, block)], sems.at[1]),
    ]
    for copy in copies:
        copy.start()
    lane = lax.broadcasted_iota(jnp.int32, (TILE, LANES), 1)
    skipped = (2 * REACH - 1) * block

    def fold(x):
        return jnp.where(x < block, jnp.maximum(x, 0), jnp.maximum(x - skipped, block))

    for copy in copies:
        copy.wait()
    for tile in range(tiles):
        own = slice(tile * TILE, (tile + 1) * TILE)
        low, high = fold(low_ref[own]), fold(high_ref[own])
        base, count = place(
            fold(bounds_ref[2 * tile]), fold(bounds_ref[2 * tile + 1]), FAR_CHUNK, span
        )
        total[...] = total_in_ref[tile]
        sums[...] = sums_in_ref[tile]

        @pl.when(count > 0)
        def _():
            before = peak_in_ref[tile]
            peak[...] = before

            def score(i):
                at = pl.multiple_of(base + i * FAR_CHUNK, LANES)
                score_chunk(
                    queries_ref[tile], window, at, FAR_CHUNK, factor, low, high, lane, scores, i, peak
                )

            loop(0, count, score)
            spread_peak(peak)
            change = jnp.exp2(before - peak[...])
            sums[...] *= change
            for j in range(latent // LANES):
                total[:, j * LANES : (j + 1) * LANES] *= change

            def weigh(i):
                at = pl.multiple_of(base + i * FAR_CHUNK, LANES)
                weigh_chunk(scores, i, window, at, FAR_CHUNK, latent, peak, sums, total)

            loop(0, count, weigh)

        share = 1.0 / jnp.sum(sums[...], axis=1, keepdims=True)
        latent_out[:, own, :] = (
            (total[...] * share).astype(jnp.bfloat16).reshape(head_count, TILE, latent)
        )
    for h in range(head_count):
        attended = jnp.dot(latent_out[h], value_ref[h], preferred_element_type=jnp.float32)
        out_ref[:, :, h * value_width : (h + 1) * value_width] = attended.astype(
            jnp.bfloat16
        ).reshape(tiles * TILE // GROUP, GROUP, value_width)


def pack(query_nope, query_rope, prompt_latent, prompt_rope, response_latent, response_rope, groups):
    bf16 = jnp.bfloat16
    width = query_nope.shape[1] + query_rope.shape[1]
    keys = prompt_latent.shape[0] + prompt_rope.shape[0]
    return pl.pallas_call(
        pack_kernel,
        out_shape=[
            jax.ShapeDtypeStruct((keys, prompt_latent.shape[1]), bf16),
            jax.ShapeDtypeStruct((groups, query_nope.shape[0], width // groups), bf16),
            jax.ShapeDtypeStruct((keys, response_latent.shape[1]), bf16),
        ],
        in_specs=[ANYWHERE] * 6,
        out_specs=[ANYWHERE] * 3,
        scratch_shapes=[pltpu.SemaphoreType.DMA((4 + 2 * groups,))],
        name="pack",
        cost_estimate=pl.CostEstimate(flops=0, bytes_accessed=4 * MIB, transcendentals=0),
    )(query_nope, query_rope, prompt_latent, prompt_rope, response_latent, response_rope)


def absorb(position, lengths, prompt_of, queries, absorb_key, rope):
    head_count, nope, latent = absorb_key.shape
    tokens = queries.shape[0]
    tiles = tokens // TILE
    limits = jax.ShapeDtypeStruct((tokens, LANES), jnp.int32)
    return pl.pallas_call(
        absorb_kernel,
        out_shape=[
            jax.ShapeDtypeStruct((tiles, head_count, TILE, latent + rope), jnp.bfloat16),
            limits,
            limits,
            jax.ShapeDtypeStruct((2 * tiles,), jnp.int32),
        ],
        in_specs=[SMEM, SMEM, VMEM, VMEM, VMEM],
        out_specs=[VMEM, VMEM, VMEM, SMEM],
        name="absorb",
        cost_estimate=pl.CostEstimate(
            flops=2 * tokens * head_count * nope * latent,
            bytes_accessed=6 * MIB,
            transcendentals=0,
        ),
        compiler_params=pltpu.CompilerParams(vmem_limit_bytes=16 * MIB),
    )(position, lengths, prompt_of, queries, absorb_key)


def attend_near(factor, position, bounds, low, high, response_start, queries, response, own, mine, theirs, latent):
    tiles, rows, width = queries.shape
    slots = -(-(2 * REACH - 1) * own.shape[1] // NEAR_CHUNK)
    span = slots * NEAR_CHUNK
    f32 = jnp.float32
    scores = pltpu.VMEM((slots, rows, NEAR_CHUNK), f32)
    return pl.pallas_call(
        lambda *refs: near_kernel(factor, *refs),
        out_shape=[
            jax.ShapeDtypeStruct((tiles, rows, latent), f32),
            jax.ShapeDtypeStruct((tiles, rows, LANES), f32),
            jax.ShapeDtypeStruct((tiles, rows, LANES), f32),
        ],
        in_specs=[SMEM, SMEM] + [VMEM] * 5 + [ANYWHERE] * 5,
        out_specs=[VMEM] * 3,
        scratch_shapes=[
            pltpu.VMEM((width, span), jnp.bfloat16),
            scores,
            scores,
            pltpu.SemaphoreType.DMA((5,)),
        ],
        name="attend_near",
        cost_estimate=pl.CostEstimate(
            flops=2 * tiles * rows * (width + latent) * 4096,
            bytes_accessed=12 * MIB,
            transcendentals=0,
        ),
        compiler_params=pltpu.CompilerParams(vmem_limit_bytes=36 * MIB),
    )(
        position, bounds, low, high, response_start, queries, response,
        own, mine[0], theirs[0], mine[1], theirs[1],
    )


def attend_far(factor, position, bounds, low, high, queries, state, value, mine, theirs):
    head_count, latent, value_width = value.shape
    tiles, rows, width = queries.shape
    block = mine.shape[1]
    f32 = jnp.float32
    return pl.pallas_call(
        lambda *refs: far_kernel(factor, *refs),
        out_shape=jax.ShapeDtypeStruct(
            (tiles * TILE // GROUP, GROUP, head_count * value_width), jnp.bfloat16
        ),
        in_specs=[SMEM, SMEM] + [VMEM] * 7 + [ANYWHERE] * 2,
        out_specs=VMEM,
        scratch_shapes=[
            pltpu.VMEM((width, 2 * block), jnp.bfloat16),
            pltpu.VMEM((2 * block // FAR_CHUNK, rows, FAR_CHUNK), f32),
            pltpu.VMEM((rows, latent), f32),
            pltpu.VMEM((rows, LANES), f32),
            pltpu.VMEM((rows, LANES), f32),
            pltpu.VMEM((head_count, tiles * TILE, latent), jnp.bfloat16),
            pltpu.SemaphoreType.DMA((2,)),
        ],
        name="attend_far",
        cost_estimate=pl.CostEstimate(
            flops=2 * tiles * rows * (width + latent) * 1024,
            bytes_accessed=12 * MIB,
            transcendentals=0,
        ),
        compiler_params=pltpu.CompilerParams(vmem_limit_bytes=28 * MIB),
    )(position, bounds, low, high, queries, *state, value, mine, theirs)


def local(
    query_nope,
    query_rope,
    absorb_key,
    value_absorption_matrix,
    prompt_latent,
    prompt_rope,
    response_latent,
    response_rope,
    prompt_lengths,
    prompt_of,
    response_start,
):
    head_count, nope_width, latent_width = absorb_key.shape
    value_width = value_absorption_matrix.shape[2]
    rope_width = prompt_rope.shape[0]
    block = prompt_latent.shape[1]
    tokens = response_latent.shape[1]
    groups = lax.axis_size("head")
    length = lax.axis_size("seq")
    seq_index = lax.axis_index("seq")
    head_index = lax.axis_index("head")
    per = tokens // groups
    factor = (nope_width + rope_width) ** (-0.5) * math.log2(math.e)

    own, sent, response = pack(
        query_nope, query_rope, prompt_latent, prompt_rope, response_latent, response_rope, groups
    )
    position = jnp.stack(
        [seq_index * tokens, head_index % 2, (seq_index - REACH) * block]
    ).astype(jnp.int32)
    starts = jnp.broadcast_to(response_start[:, None], (tokens, LANES))
    prompts = jnp.broadcast_to(prompt_of[:, None], (tokens, LANES))

    onward = [
        (i * groups + h, (i + by) * groups + h)
        for i in range(length)
        for h in range(groups)
        for by in (1 - 2 * (h % 2),)
        if 0 <= i + by < length
    ]
    swapped = [(h, h ^ 1) for h in range(groups)]

    arrived = lax.all_to_all(sent, "head", split_axis=0, concat_axis=0, tiled=True)
    queries, low, high, bounds = absorb(
        position,
        prompt_lengths,
        prompts,
        arrived.reshape(tokens, head_count * (nope_width + rope_width)),
        absorb_key,
        rope_width,
    )
    queries = queries.reshape(tokens // TILE, head_count * TILE, latent_width + rope_width)

    first = lax.ppermute(own, ("seq", "head"), onward)
    first, queries = lax.optimization_barrier((first, queries))
    second = lax.ppermute(first, ("seq", "head"), onward)
    third = lax.ppermute(second, ("seq", "head"), onward)
    near = [first, second]
    swaps = [lax.ppermute(held, "head", swapped) for held in near]

    state = attend_near(
        factor, position, bounds, low, high, starts, queries, response, own, near, swaps, latent_width
    )
    third, state = lax.optimization_barrier((third, state))
    attended = attend_far(
        factor, position, bounds, low, high, queries, state, value_absorption_matrix,
        third, lax.ppermute(third, "head", swapped),
    )
    returned = lax.all_to_all(attended, "head", split_axis=0, concat_axis=0, tiled=True)
    return returned.transpose(1, 0, 2).reshape(per, groups * head_count * value_width)


def solution(mesh):
    return jax.shard_map(
        local,
        mesh=mesh,
        in_specs=(
            P(("seq", "head"), None),
            P(("seq", "head"), None),
            P("head", None, None),
            P("head", None, None),
            P(None, "seq"),
            P(None, "seq"),
            P(None, "seq"),
            P(None, "seq"),
            P(),
            P("seq"),
            P("seq"),
        ),
        out_specs=P(("seq", "head"), None),
        check_vma=False,
    )
```

```python
import math

import jax
import jax.numpy as jnp
from jax import lax
from jax.experimental import pallas as pl
from jax.experimental.pallas import tpu as pltpu
from jax.sharding import PartitionSpec as P

PMAX = 2304
REACH = 3
GROUP = 16
TILE = 32
LANES = 128
OWN_CHUNK = 512
NEAR_CHUNK = 512
FAR_CHUNK = 384
NEG = -1e30
MIB = 1024 * 1024

VMEM = pl.BlockSpec(memory_space=pltpu.VMEM)
SMEM = pl.BlockSpec(memory_space=pltpu.SMEM)
ANYWHERE = pl.BlockSpec(memory_space=pl.ANY)


def pack_kernel(
    nope_ref,
    rope_ref,
    latent_ref,
    key_rope_ref,
    response_latent_ref,
    response_rope_ref,
    own_ref,
    sent_ref,
    response_ref,
):
    latent = latent_ref.shape[0]
    groups, _, width = sent_ref.shape
    nope = nope_ref.shape[1] // groups
    rope = rope_ref.shape[1] // groups
    own_ref[:latent, :] = latent_ref[...]
    own_ref[latent:, :] = key_rope_ref[...]
    response_ref[:latent, :] = response_latent_ref[...]
    response_ref[latent:, :] = response_rope_ref[...]
    for g in range(groups):
        sent_ref[g, :, :nope] = nope_ref[:, g * nope : (g + 1) * nope]
        sent_ref[g, :, nope:] = rope_ref[:, g * rope : (g + 1) * rope]


def absorb_kernel(
    position_ref,
    lengths_ref,
    prompt_lane_ref,
    start_lane_ref,
    prompt_row_ref,
    queries_ref,
    absorb_ref,
    out_ref,
    limits_ref,
    order_ref,
    bounds_ref,
):
    head_count, nope, latent = absorb_ref.shape
    tokens = queries_ref.shape[0]
    tiles = tokens // TILE
    rope = out_ref.shape[3] - latent
    by_lane = prompt_lane_ref[...]
    by_row = prompt_row_ref[...]
    row = lax.broadcasted_iota(jnp.int32, (tokens, tokens), 0)
    lane = lax.broadcasted_iota(jnp.int32, (tokens, tokens), 1)
    ahead = (by_row < by_lane) | ((by_row == by_lane) & (row < lane))
    rank = jnp.sum(ahead.astype(jnp.int32), axis=0, keepdims=True)
    chosen = row == rank
    order = chosen.astype(jnp.float32).astype(jnp.bfloat16)
    order_ref[...] = order

    low = jnp.zeros_like(by_lane)
    high = jnp.zeros_like(by_lane)
    start = -position_ref[2]
    for p in range(lengths_ref.shape[0]):
        here = by_lane == p
        end = start + lengths_ref[p]
        low = jnp.where(here, start, low)
        high = jnp.where(here, end, high)
        start = end
    for i, values in enumerate(
        (low, high, start_lane_ref[...] - position_ref[0], lane[:1])
    ):
        sorted_values = jnp.sum(jnp.where(chosen, values, 0), axis=1, keepdims=True)
        limits_ref[i] = jnp.broadcast_to(sorted_values, (tokens, LANES))
    for tile in range(tiles):
        own = slice(tile * TILE, (tile + 1) * TILE)
        bounds_ref[2 * tile] = jnp.min(limits_ref[0, own, :1])
        bounds_ref[2 * tile + 1] = jnp.max(limits_ref[1, own, :1])

    queries = jnp.dot(order, queries_ref[...], preferred_element_type=jnp.float32)
    queries = queries.astype(jnp.bfloat16)
    for h in range(head_count):
        part = jnp.dot(
            queries[:, h * nope : (h + 1) * nope],
            absorb_ref[h],
            preferred_element_type=jnp.float32,
        ).astype(jnp.bfloat16)
        out_ref[:, h, :, :latent] = part.reshape(tiles, TILE, latent)
        first = head_count * nope + h * rope
        out_ref[:, h, :, latent:] = queries[:, first : first + rope].reshape(tiles, TILE, rope)


def place(least, most, chunk, span):
    base = least // LANES * LANES
    count = (most - base + chunk - 1) // chunk
    return jnp.minimum(base, span - count * chunk), count


def masked(part, factor, allowed):
    rows, columns = part.shape
    shaped = (part * factor).reshape(rows // TILE, TILE, columns)
    return jnp.where(allowed[None], shaped, NEG).reshape(rows, columns)


def loop(first, last, body):
    @pl.loop(first, last)
    def _(i):
        body(i)


def score_chunk(queries, window, at, chunk, factor, low, high, lane, scores, slot, peak):
    values = jnp.dot(queries, window[:, pl.ds(at, chunk)], preferred_element_type=jnp.float32)
    largest = peak[...]
    for j in range(chunk // LANES):
        column = lane + (at + j * LANES)
        part = values[:, j * LANES : (j + 1) * LANES]
        part = masked(part, factor, (column >= low) & (column < high))
        scores[slot, :, j * LANES : (j + 1) * LANES] = part
        largest = jnp.maximum(largest, part)
    peak[...] = largest


def weigh_chunk(scores, slot, window, at, chunk, latent, peak, sums, total):
    peak = peak[...]
    parts = [
        jnp.exp2(scores[slot, :, j * LANES : (j + 1) * LANES] - peak) for j in range(chunk // LANES)
    ]
    weights = jnp.concatenate([part.astype(jnp.bfloat16) for part in parts], axis=1)
    total[...] += lax.dot_general(
        weights,
        window[:latent, pl.ds(at, chunk)],
        (((1,), (1,)), ((), ())),
        preferred_element_type=jnp.float32,
    )
    added = parts[0]
    for part in parts[1:]:
        added = added + part
    sums[...] += added


def spread_peak(peak):
    peak[...] = jnp.broadcast_to(jnp.max(peak[...], axis=1, keepdims=True), peak.shape)


def fill(window, pairs, sems):
    copies = []
    for i, (keys, at) in enumerate(pairs):
        target = window.at[:, pl.ds(pl.multiple_of(at, LANES), keys.shape[1])]
        copies.append(pltpu.make_async_copy(keys, target, sems.at[i]))
    for copy in copies:
        copy.start()
    return copies


def zero_tail(window, filled):
    rows, span = window.shape
    if span > filled:
        window[:, filled:] = jnp.zeros((rows, span - filled), window.dtype)


def run_tiles(
    factor, fold, chunk, limits_ref, bounds_ref, queries_ref, window, scores, state, wait, begin, skip
):
    total_ref, peak_ref, sums_ref = state
    tiles = queries_ref.shape[0]
    latent = total_ref.shape[2]
    span = window.shape[1]
    lane = lax.broadcasted_iota(jnp.int32, (TILE, LANES), 1)
    places = [
        place(fold(bounds_ref[2 * tile]), fold(bounds_ref[2 * tile + 1]), chunk, span)
        for tile in range(tiles)
    ]

    def score(tile, i):
        own = slice(tile * TILE, (tile + 1) * TILE)
        at = pl.multiple_of(places[tile][0] + i * chunk, LANES)
        score_chunk(
            queries_ref[tile],
            window,
            at,
            chunk,
            factor,
            fold(limits_ref[0, own]),
            fold(limits_ref[1, own]),
            lane,
            scores[tile % 2],
            i,
            peak_ref.at[tile],
        )

    def weigh(tile, i):
        at = pl.multiple_of(places[tile][0] + i * chunk, LANES)
        weigh_chunk(
            scores[tile % 2],
            i,
            window,
            at,
            chunk,
            latent,
            peak_ref.at[tile],
            sums_ref.at[tile],
            total_ref.at[tile],
        )

    wait()
    loop(0, places[0][1], lambda i: score(0, i))
    for tile in range(tiles):
        count = places[tile][1]
        if skip:

            @pl.when(count > 0)
            def _():
                begin(tile)

        else:
            begin(tile)
        if tile + 1 < tiles:
            following = places[tile + 1][1]
            both = jnp.minimum(count, following)

            def fused(i):
                weigh(tile, i)
                score(tile + 1, i)

            loop(0, both, fused)
            loop(both, following, lambda i: score(tile + 1, i))
            loop(both, count, lambda i: weigh(tile, i))
        else:
            loop(0, count, lambda i: weigh(tile, i))


def rescale(before, peak, sums, total):
    change = jnp.exp2(before - peak[...])
    sums[...] *= change
    for at in range(0, total.shape[1], LANES):
        total[:, at : at + LANES] *= change


def own_kernel(
    factor,
    bounds_ref,
    limits_ref,
    queries_ref,
    response_ref,
    own_ref,
    total_ref,
    peak_ref,
    sums_ref,
    window,
    scores_even,
    scores_odd,
    sems,
):
    block = own_ref.shape[1]
    tiles, rows, width = queries_ref.shape
    latent = total_ref.shape[2]
    copies = fill(window, [(own_ref, 0)], sems)
    zero_tail(window, block)
    lane = lax.broadcasted_iota(jnp.int32, (TILE, LANES), 1)
    all_rows = queries_ref[...].reshape(tiles * rows, width)
    own_scores = jnp.dot(all_rows, response_ref[...], preferred_element_type=jnp.float32)
    for tile in range(tiles):
        own = slice(tile * TILE, (tile + 1) * TILE)
        causal = (lane >= limits_ref[2, own]) & (lane <= limits_ref[3, own])
        part = masked(own_scores[tile * rows : (tile + 1) * rows], factor, causal)
        sums_ref[tile] = part
        peak_ref[tile] = part

    def begin(tile):
        spread_peak(peak_ref.at[tile])
        weights = jnp.exp2(sums_ref[tile] - peak_ref[tile])
        sums_ref[tile] = weights
        total_ref[tile] = lax.dot_general(
            weights.astype(jnp.bfloat16),
            response_ref[:latent, :],
            (((1,), (1,)), ((), ())),
            preferred_element_type=jnp.float32,
        )

    def wait():
        for copy in copies:
            copy.wait()

    run_tiles(
        factor,
        lambda x: jnp.clip(x - REACH * block, 0, block),
        OWN_CHUNK,
        limits_ref,
        bounds_ref,
        queries_ref,
        window,
        (scores_even, scores_odd),
        (total_ref, peak_ref, sums_ref),
        wait,
        begin,
        False,
    )


def near_kernel(
    factor,
    position_ref,
    bounds_ref,
    limits_ref,
    queries_ref,
    total_in_ref,
    peak_in_ref,
    sums_in_ref,
    mine1_ref,
    theirs1_ref,
    mine2_ref,
    theirs2_ref,
    total_ref,
    peak_ref,
    sums_ref,
    window,
    scores_even,
    scores_odd,
    sems,
):
    block = mine1_ref.shape[1]
    core = position_ref[1]
    copies = fill(
        window,
        [
            (mine1_ref, (1 + core) * block),
            (theirs1_ref, (2 - core) * block),
            (mine2_ref, 3 * core * block),
            (theirs2_ref, (3 - 3 * core) * block),
        ],
        sems,
    )
    total_ref[...] = total_in_ref[...]
    peak_ref[...] = peak_in_ref[...]
    sums_ref[...] = sums_in_ref[...]

    def fold(x):
        return jnp.where(
            x < REACH * block,
            jnp.maximum(x - block, 0),
            jnp.clip(x - 2 * block, 2 * block, 4 * block),
        )

    def begin(tile):
        spread_peak(peak_ref.at[tile])
        rescale(peak_in_ref[tile], peak_ref.at[tile], sums_ref.at[tile], total_ref.at[tile])

    def wait():
        for copy in copies:
            copy.wait()

    run_tiles(
        factor,
        fold,
        NEAR_CHUNK,
        limits_ref,
        bounds_ref,
        queries_ref,
        window,
        (scores_even, scores_odd),
        (total_ref, peak_ref, sums_ref),
        wait,
        begin,
        True,
    )


def far_kernel(
    factor,
    position_ref,
    bounds_ref,
    limits_ref,
    queries_ref,
    total_in_ref,
    peak_in_ref,
    sums_in_ref,
    value_ref,
    order_ref,
    mine_ref,
    theirs_ref,
    out_ref,
    window,
    scores_even,
    scores_odd,
    total,
    peak,
    sums,
    latent_out,
    sems,
):
    block = mine_ref.shape[1]
    tiles, rows, _ = queries_ref.shape
    head_count, latent, value_width = value_ref.shape
    core = position_ref[1]
    copies = fill(window, [(mine_ref, core * block), (theirs_ref, (1 - core) * block)], sems)
    skipped = (2 * REACH - 1) * block

    def fold(x):
        return jnp.where(x < block, jnp.maximum(x, 0), jnp.maximum(x - skipped, block))

    total[...] = total_in_ref[...]
    peak[...] = peak_in_ref[...]
    sums[...] = sums_in_ref[...]

    def begin(tile):
        spread_peak(peak.at[tile])
        rescale(peak_in_ref[tile], peak.at[tile], sums.at[tile], total.at[tile])

    def wait():
        for copy in copies:
            copy.wait()

    run_tiles(
        factor,
        fold,
        FAR_CHUNK,
        limits_ref,
        bounds_ref,
        queries_ref,
        window,
        (scores_even, scores_odd),
        (total, peak, sums),
        wait,
        begin,
        True,
    )
    for tile in range(tiles):
        own = slice(tile * TILE, (tile + 1) * TILE)
        share = 1.0 / jnp.sum(sums[tile], axis=1, keepdims=True)
        latent_out[:, own, :] = (
            (total[tile] * share).astype(jnp.bfloat16).reshape(head_count, TILE, latent)
        )
    order = order_ref[...]
    for h in range(head_count):
        attended = jnp.dot(latent_out[h], value_ref[h], preferred_element_type=jnp.float32)
        attended = lax.dot_general(
            order,
            attended.astype(jnp.bfloat16),
            (((0,), (0,)), ((), ())),
            preferred_element_type=jnp.float32,
        )
        out_ref[:, :, h * value_width : (h + 1) * value_width] = attended.astype(
            jnp.bfloat16
        ).reshape(tiles * TILE // GROUP, GROUP, value_width)


def pack(query_nope, query_rope, prompt_latent, prompt_rope, response_latent, response_rope, groups):
    bf16 = jnp.bfloat16
    width = query_nope.shape[1] + query_rope.shape[1]
    keys = prompt_latent.shape[0] + prompt_rope.shape[0]
    return pl.pallas_call(
        pack_kernel,
        out_shape=[
            jax.ShapeDtypeStruct((keys, prompt_latent.shape[1]), bf16),
            jax.ShapeDtypeStruct((groups, query_nope.shape[0], width // groups), bf16),
            jax.ShapeDtypeStruct((keys, response_latent.shape[1]), bf16),
        ],
        in_specs=[VMEM] * 6,
        out_specs=[VMEM] * 3,
        name="pack",
        cost_estimate=pl.CostEstimate(flops=0, bytes_accessed=4 * MIB, transcendentals=0),
    )(query_nope, query_rope, prompt_latent, prompt_rope, response_latent, response_rope)


def absorb(position, lengths, prompt_of, response_start, queries, absorb_key, rope):
    head_count, nope, latent = absorb_key.shape
    tokens = queries.shape[0]
    tiles = tokens // TILE
    return pl.pallas_call(
        absorb_kernel,
        out_shape=[
            jax.ShapeDtypeStruct((tiles, head_count, TILE, latent + rope), jnp.bfloat16),
            jax.ShapeDtypeStruct((4, tokens, LANES), jnp.int32),
            jax.ShapeDtypeStruct((tokens, tokens), jnp.bfloat16),
            jax.ShapeDtypeStruct((2 * tiles,), jnp.int32),
        ],
        in_specs=[SMEM, SMEM] + [VMEM] * 5,
        out_specs=[VMEM, VMEM, VMEM, SMEM],
        name="absorb",
        cost_estimate=pl.CostEstimate(
            flops=2 * tokens * head_count * nope * latent,
            bytes_accessed=6 * MIB,
            transcendentals=0,
        ),
        compiler_params=pltpu.CompilerParams(vmem_limit_bytes=16 * MIB),
    )(
        position,
        lengths,
        prompt_of.reshape(1, tokens),
        response_start.reshape(1, tokens),
        jnp.broadcast_to(prompt_of[:, None], (tokens, tokens)),
        queries,
        absorb_key,
    )


def state_shapes(tiles, rows, latent):
    f32 = jnp.float32
    return [
        jax.ShapeDtypeStruct((tiles, rows, latent), f32),
        jax.ShapeDtypeStruct((tiles, rows, LANES), f32),
        jax.ShapeDtypeStruct((tiles, rows, LANES), f32),
    ]


def key_scratch(width, columns, rows, chunk, copies):
    slots = -(-columns // chunk)
    scores = pltpu.VMEM((slots, rows, chunk), jnp.float32)
    window = pltpu.VMEM((width, slots * chunk), jnp.bfloat16)
    return window, scores, scores, pltpu.SemaphoreType.DMA((copies,))


def cost(queries, latent, columns):
    tiles, rows, width = queries.shape
    return pl.CostEstimate(
        flops=2 * tiles * rows * (width + latent) * columns,
        bytes_accessed=4 * MIB,
        transcendentals=tiles * rows * columns,
    )


def attend_own(factor, bounds, limits, queries, response, own, latent):
    tiles, rows, width = queries.shape
    block = own.shape[1]
    return pl.pallas_call(
        lambda *refs: own_kernel(factor, *refs),
        out_shape=state_shapes(tiles, rows, latent),
        in_specs=[SMEM] + [VMEM] * 3 + [ANYWHERE],
        out_specs=[VMEM] * 3,
        scratch_shapes=list(key_scratch(width, block, rows, OWN_CHUNK, 1)),
        name="attend_own",
        cost_estimate=cost(queries, latent, block),
        compiler_params=pltpu.CompilerParams(vmem_limit_bytes=16 * MIB),
    )(bounds, limits, queries, response, own)


def attend_near(factor, position, bounds, limits, queries, state, mine, theirs):
    tiles, rows, width = queries.shape
    latent = state[0].shape[2]
    block = mine[0].shape[1]
    return pl.pallas_call(
        lambda *refs: near_kernel(factor, *refs),
        out_shape=state_shapes(tiles, rows, latent),
        in_specs=[SMEM, SMEM] + [VMEM] * 5 + [ANYWHERE] * 4,
        out_specs=[VMEM] * 3,
        scratch_shapes=list(key_scratch(width, 4 * block, rows, NEAR_CHUNK, 4)),
        input_output_aliases={4: 0},
        name="attend_near",
        cost_estimate=cost(queries, latent, 2 * block),
        compiler_params=pltpu.CompilerParams(vmem_limit_bytes=24 * MIB),
    )(position, bounds, limits, queries, *state, mine[0], theirs[0], mine[1], theirs[1])


def attend_far(factor, position, bounds, limits, queries, state, value, order, mine, theirs):
    head_count, latent, value_width = value.shape
    tiles, rows, width = queries.shape
    block = mine.shape[1]
    f32 = jnp.float32
    window, even, odd, sems = key_scratch(width, 2 * block, rows, FAR_CHUNK, 2)
    return pl.pallas_call(
        lambda *refs: far_kernel(factor, *refs),
        out_shape=jax.ShapeDtypeStruct(
            (tiles * TILE // GROUP, GROUP, head_count * value_width), jnp.bfloat16
        ),
        in_specs=[SMEM, SMEM] + [VMEM] * 7 + [ANYWHERE] * 2,
        out_specs=VMEM,
        scratch_shapes=[
            window,
            even,
            odd,
            pltpu.VMEM((tiles, rows, latent), f32),
            pltpu.VMEM((tiles, rows, LANES), f32),
            pltpu.VMEM((tiles, rows, LANES), f32),
            pltpu.VMEM((head_count, tiles * TILE, latent), jnp.bfloat16),
            sems,
        ],
        name="attend_far",
        cost_estimate=cost(queries, latent, block),
        compiler_params=pltpu.CompilerParams(vmem_limit_bytes=24 * MIB),
    )(position, bounds, limits, queries, *state, value, order, mine, theirs)


def local(
    query_nope,
    query_rope,
    absorb_key,
    value_absorption_matrix,
    prompt_latent,
    prompt_rope,
    response_latent,
    response_rope,
    prompt_lengths,
    prompt_of,
    response_start,
):
    head_count, nope_width, latent_width = absorb_key.shape
    value_width = value_absorption_matrix.shape[2]
    rope_width = prompt_rope.shape[0]
    block = prompt_latent.shape[1]
    tokens = response_latent.shape[1]
    groups = lax.axis_size("head")
    length = lax.axis_size("seq")
    seq_index = lax.axis_index("seq")
    head_index = lax.axis_index("head")
    per = tokens // groups
    factor = (nope_width + rope_width) ** (-0.5) * math.log2(math.e)

    own, sent, response = pack(
        query_nope, query_rope, prompt_latent, prompt_rope, response_latent, response_rope, groups
    )
    position = jnp.stack(
        [seq_index * tokens, head_index % 2, (seq_index - REACH) * block]
    ).astype(jnp.int32)
    onward = [
        (i * groups + h, (i + by) * groups + h)
        for i in range(length)
        for h in range(groups)
        for by in (1 - 2 * (h % 2),)
        if 0 <= i + by < length
    ]
    swapped = [(h, h ^ 1) for h in range(groups)]

    arrived = lax.all_to_all(sent, "head", split_axis=0, concat_axis=0, tiled=True)
    queries, limits, order, bounds = absorb(
        position,
        prompt_lengths,
        prompt_of,
        response_start,
        arrived.reshape(tokens, head_count * (nope_width + rope_width)),
        absorb_key,
        rope_width,
    )
    queries = queries.reshape(tokens // TILE, head_count * TILE, latent_width + rope_width)

    first = lax.ppermute(own, ("seq", "head"), onward)
    first, queries = lax.optimization_barrier((first, queries))
    second = lax.ppermute(first, ("seq", "head"), onward)
    state = attend_own(factor, bounds, limits, queries, response, own, latent_width)
    second, state = lax.optimization_barrier((second, state))
    third = lax.ppermute(second, ("seq", "head"), onward)
    near = [first, second]
    swaps = [lax.ppermute(held, "head", swapped) for held in near]
    state = attend_near(factor, position, bounds, limits, queries, state, near, swaps)
    third, state = lax.optimization_barrier((third, state))
    attended = attend_far(
        factor,
        position,
        bounds,
        limits,
        queries,
        state,
        value_absorption_matrix,
        order,
        third,
        lax.ppermute(third, "head", swapped),
    )
    returned = lax.all_to_all(attended, "head", split_axis=0, concat_axis=0, tiled=True)
    return returned.transpose(1, 0, 2).reshape(per, groups * head_count * value_width)


def solution(mesh):
    return jax.shard_map(
        local,
        mesh=mesh,
        in_specs=(
            P(("seq", "head"), None),
            P(("seq", "head"), None),
            P("head", None, None),
            P("head", None, None),
            P(None, "seq"),
            P(None, "seq"),
            P(None, "seq"),
            P(None, "seq"),
            P(),
            P("seq"),
            P("seq"),
        ),
        out_specs=P(("seq", "head"), None),
        check_vma=False,
    )
```

```python
import math

import jax
import jax.numpy as jnp
from jax import lax
from jax.experimental import pallas as pl
from jax.experimental.pallas import tpu as pltpu
from jax.sharding import PartitionSpec as P

PMAX = 2304
REACH = 3
GROUP = 16
TILE = 32
LANES = 128
SMALL = 256
BIG = 3 * SMALL
NEG = -1e30
MIB = 1024 * 1024

VMEM = pl.BlockSpec(memory_space=pltpu.VMEM)
SMEM = pl.BlockSpec(memory_space=pltpu.SMEM)
ANYWHERE = pl.BlockSpec(memory_space=pl.ANY)


def pack_kernel(
    nope_ref,
    rope_ref,
    latent_ref,
    key_rope_ref,
    response_latent_ref,
    response_rope_ref,
    own_ref,
    sent_ref,
    response_ref,
):
    latent = latent_ref.shape[0]
    groups, _, width = sent_ref.shape
    nope = nope_ref.shape[1] // groups
    rope = rope_ref.shape[1] // groups
    own_ref[:latent, :] = latent_ref[...]
    own_ref[latent:, :] = key_rope_ref[...]
    response_ref[:latent, :] = response_latent_ref[...]
    response_ref[latent:, :] = response_rope_ref[...]
    for g in range(groups):
        sent_ref[g, :, :nope] = nope_ref[:, g * nope : (g + 1) * nope]
        sent_ref[g, :, nope:] = rope_ref[:, g * rope : (g + 1) * rope]


def absorb_kernel(
    position_ref,
    lengths_ref,
    prompt_lane_ref,
    start_lane_ref,
    prompt_row_ref,
    queries_ref,
    absorb_ref,
    out_ref,
    limits_ref,
    order_ref,
    bounds_ref,
):
    head_count, nope, latent = absorb_ref.shape
    tokens = queries_ref.shape[0]
    tiles = tokens // TILE
    rope = out_ref.shape[3] - latent
    by_lane = prompt_lane_ref[...]
    by_row = prompt_row_ref[...]
    row = lax.broadcasted_iota(jnp.int32, (tokens, tokens), 0)
    lane = lax.broadcasted_iota(jnp.int32, (tokens, tokens), 1)
    ahead = (by_row < by_lane) | ((by_row == by_lane) & (row < lane))
    rank = jnp.sum(ahead.astype(jnp.int32), axis=0, keepdims=True)
    chosen = row == rank
    order = chosen.astype(jnp.float32).astype(jnp.bfloat16)
    order_ref[...] = order

    low = jnp.zeros_like(by_lane)
    high = jnp.zeros_like(by_lane)
    start = -position_ref[2]
    for p in range(lengths_ref.shape[0]):
        here = by_lane == p
        end = start + lengths_ref[p]
        low = jnp.where(here, start, low)
        high = jnp.where(here, end, high)
        start = end
    for i, values in enumerate(
        (low, high, start_lane_ref[...] - position_ref[0], lane[:1])
    ):
        sorted_values = jnp.sum(jnp.where(chosen, values, 0), axis=1, keepdims=True)
        limits_ref[i] = jnp.broadcast_to(sorted_values, (tokens, LANES))
    for tile in range(tiles):
        own = slice(tile * TILE, (tile + 1) * TILE)
        bounds_ref[2 * tile] = jnp.min(limits_ref[0, own, :1])
        bounds_ref[2 * tile + 1] = jnp.max(limits_ref[1, own, :1])

    queries = jnp.dot(order, queries_ref[...], preferred_element_type=jnp.float32)
    queries = queries.astype(jnp.bfloat16)
    for h in range(head_count):
        part = jnp.dot(
            queries[:, h * nope : (h + 1) * nope],
            absorb_ref[h],
            preferred_element_type=jnp.float32,
        ).astype(jnp.bfloat16)
        out_ref[:, h, :, :latent] = part.reshape(tiles, TILE, latent)
        first = head_count * nope + h * rope
        out_ref[:, h, :, latent:] = queries[:, first : first + rope].reshape(tiles, TILE, rope)


def place(least, most, span):
    base = least // LANES * LANES
    count = (most - base + SMALL - 1) // SMALL
    return jnp.minimum(base, span - count * SMALL), count


def masked(part, factor, allowed):
    rows, columns = part.shape
    shaped = (part * factor).reshape(rows // TILE, TILE, columns)
    return jnp.where(allowed[None], shaped, NEG).reshape(rows, columns)


def loop(first, last, body):
    @pl.loop(first, last)
    def _(i):
        body(i)


def score_chunk(queries, window, at, slot, count, factor, low, high, lane, scores, peak):
    values = jnp.dot(
        queries, window[:, pl.ds(at, count * SMALL)], preferred_element_type=jnp.float32
    )
    largest = peak[...]
    for j in range(count * SMALL // LANES):
        column = lane + (at + j * LANES)
        part = values[:, j * LANES : (j + 1) * LANES]
        part = masked(part, factor, (column >= low) & (column < high))
        first = j * LANES % SMALL
        scores[slot + j * LANES // SMALL, :, first : first + LANES] = part
        largest = jnp.maximum(largest, part)
    peak[...] = largest


def weigh_chunk(scores, window, at, slot, count, latent, peak, sums, total):
    peak = peak[...]
    parts = []
    for j in range(count * SMALL // LANES):
        first = j * LANES % SMALL
        parts.append(
            jnp.exp2(scores[slot + j * LANES // SMALL, :, first : first + LANES] - peak)
        )
    weights = jnp.concatenate([part.astype(jnp.bfloat16) for part in parts], axis=1)
    total[...] += lax.dot_general(
        weights,
        window[:latent, pl.ds(at, count * SMALL)],
        (((1,), (1,)), ((), ())),
        preferred_element_type=jnp.float32,
    )
    added = parts[0]
    for part in parts[1:]:
        added = added + part
    sums[...] += added


def spread_peak(peak):
    peak[...] = jnp.broadcast_to(jnp.max(peak[...], axis=1, keepdims=True), peak.shape)


def fill(window, pairs, sems):
    copies = []
    for i, (keys, at) in enumerate(pairs):
        target = window.at[:, pl.ds(pl.multiple_of(at, LANES), keys.shape[1])]
        copies.append(pltpu.make_async_copy(keys, target, sems.at[i]))
    for copy in copies:
        copy.start()
    return copies


def run_tiles(
    factor, fold, limits_ref, bounds_ref, queries_ref, window, scores, state, wait, begin, skip
):
    total_ref, peak_ref, sums_ref = state
    tiles = queries_ref.shape[0]
    latent = total_ref.shape[2]
    span = window.shape[1]
    lane = lax.broadcasted_iota(jnp.int32, (TILE, LANES), 1)
    places = [
        place(fold(bounds_ref[2 * tile]), fold(bounds_ref[2 * tile + 1]), span)
        for tile in range(tiles)
    ]
    per = BIG // SMALL

    def score(tile, slot, count):
        own = slice(tile * TILE, (tile + 1) * TILE)
        at = pl.multiple_of(places[tile][0] + slot * SMALL, LANES)
        score_chunk(
            queries_ref[tile],
            window,
            at,
            slot,
            count,
            factor,
            fold(limits_ref[0, own]),
            fold(limits_ref[1, own]),
            lane,
            scores[tile % 2],
            peak_ref.at[tile],
        )

    def weigh(tile, slot, count):
        at = pl.multiple_of(places[tile][0] + slot * SMALL, LANES)
        weigh_chunk(
            scores[tile % 2],
            window,
            at,
            slot,
            count,
            latent,
            peak_ref.at[tile],
            sums_ref.at[tile],
            total_ref.at[tile],
        )

    def rest(tile, done, body):
        count = places[tile][1]
        bigs = count // per
        loop(done, bigs, lambda i: body(tile, i * per, per))
        loop(bigs * per, count, lambda i: body(tile, i, 1))

    wait()
    rest(0, 0, score)
    for tile in range(tiles):
        count = places[tile][1]
        if skip:

            @pl.when(count > 0)
            def _():
                begin(tile)

        else:
            begin(tile)
        if tile + 1 < tiles:
            both = jnp.minimum(count, places[tile + 1][1]) // per

            def fused(i):
                weigh(tile, i * per, per)
                score(tile + 1, i * per, per)

            loop(0, both, fused)
            rest(tile + 1, both, score)
            rest(tile, both, weigh)
        else:
            rest(tile, 0, weigh)


def rescale(before, peak, sums, total):
    change = jnp.exp2(before - peak[...])
    sums[...] *= change
    for at in range(0, total.shape[1], LANES):
        total[:, at : at + LANES] *= change


def own_kernel(
    factor,
    bounds_ref,
    limits_ref,
    queries_ref,
    response_ref,
    own_ref,
    total_ref,
    peak_ref,
    sums_ref,
    window,
    scores_even,
    scores_odd,
    sems,
):
    block = own_ref.shape[1]
    tiles, rows, width = queries_ref.shape
    latent = total_ref.shape[2]
    copies = fill(window, [(own_ref, 0)], sems)
    lane = lax.broadcasted_iota(jnp.int32, (TILE, LANES), 1)
    all_rows = queries_ref[...].reshape(tiles * rows, width)
    own_scores = jnp.dot(all_rows, response_ref[...], preferred_element_type=jnp.float32)
    for tile in range(tiles):
        own = slice(tile * TILE, (tile + 1) * TILE)
        causal = (lane >= limits_ref[2, own]) & (lane <= limits_ref[3, own])
        part = masked(own_scores[tile * rows : (tile + 1) * rows], factor, causal)
        sums_ref[tile] = part
        peak_ref[tile] = part

    def begin(tile):
        spread_peak(peak_ref.at[tile])
        weights = jnp.exp2(sums_ref[tile] - peak_ref[tile])
        sums_ref[tile] = weights
        total_ref[tile] = lax.dot_general(
            weights.astype(jnp.bfloat16),
            response_ref[:latent, :],
            (((1,), (1,)), ((), ())),
            preferred_element_type=jnp.float32,
        )

    def wait():
        for copy in copies:
            copy.wait()

    run_tiles(
        factor,
        lambda x: jnp.clip(x - REACH * block, 0, block),
        limits_ref,
        bounds_ref,
        queries_ref,
        window,
        (scores_even, scores_odd),
        (total_ref, peak_ref, sums_ref),
        wait,
        begin,
        False,
    )


def near_kernel(
    factor,
    position_ref,
    bounds_ref,
    limits_ref,
    queries_ref,
    total_in_ref,
    peak_in_ref,
    sums_in_ref,
    mine1_ref,
    theirs1_ref,
    mine2_ref,
    theirs2_ref,
    total_ref,
    peak_ref,
    sums_ref,
    window,
    scores_even,
    scores_odd,
    sems,
):
    block = mine1_ref.shape[1]
    core = position_ref[1]
    copies = fill(
        window,
        [
            (mine1_ref, (1 + core) * block),
            (theirs1_ref, (2 - core) * block),
            (mine2_ref, 3 * core * block),
            (theirs2_ref, (3 - 3 * core) * block),
        ],
        sems,
    )
    total_ref[...] = total_in_ref[...]
    peak_ref[...] = peak_in_ref[...]
    sums_ref[...] = sums_in_ref[...]

    def fold(x):
        return jnp.where(
            x < REACH * block,
            jnp.maximum(x - block, 0),
            jnp.clip(x - 2 * block, 2 * block, 4 * block),
        )

    def begin(tile):
        spread_peak(peak_ref.at[tile])
        rescale(peak_in_ref[tile], peak_ref.at[tile], sums_ref.at[tile], total_ref.at[tile])

    def wait():
        for copy in copies:
            copy.wait()

    run_tiles(
        factor,
        fold,
        limits_ref,
        bounds_ref,
        queries_ref,
        window,
        (scores_even, scores_odd),
        (total_ref, peak_ref, sums_ref),
        wait,
        begin,
        True,
    )


def far_kernel(
    factor,
    position_ref,
    bounds_ref,
    limits_ref,
    queries_ref,
    total_in_ref,
    peak_in_ref,
    sums_in_ref,
    value_ref,
    order_ref,
    mine_ref,
    theirs_ref,
    out_ref,
    window,
    scores_even,
    scores_odd,
    total,
    peak,
    sums,
    latent_out,
    attended,
    sems,
):
    block = mine_ref.shape[1]
    tiles, rows, _ = queries_ref.shape
    head_count, latent, value_width = value_ref.shape
    core = position_ref[1]
    copies = fill(window, [(mine_ref, core * block), (theirs_ref, (1 - core) * block)], sems)
    skipped = (2 * REACH - 1) * block

    def fold(x):
        return jnp.where(x < block, jnp.maximum(x, 0), jnp.maximum(x - skipped, block))

    total[...] = total_in_ref[...]
    peak[...] = peak_in_ref[...]
    sums[...] = sums_in_ref[...]

    def begin(tile):
        spread_peak(peak.at[tile])
        rescale(peak_in_ref[tile], peak.at[tile], sums.at[tile], total.at[tile])

    def wait():
        for copy in copies:
            copy.wait()

    run_tiles(
        factor,
        fold,
        limits_ref,
        bounds_ref,
        queries_ref,
        window,
        (scores_even, scores_odd),
        (total, peak, sums),
        wait,
        begin,
        True,
    )
    for tile in range(tiles):
        own = slice(tile * TILE, (tile + 1) * TILE)
        share = 1.0 / jnp.sum(sums[tile], axis=1, keepdims=True)
        latent_out[:, own, :] = (
            (total[tile] * share).astype(jnp.bfloat16).reshape(head_count, TILE, latent)
        )
    for h in range(head_count):
        attended[:, h * value_width : (h + 1) * value_width] = jnp.dot(
            latent_out[h], value_ref[h], preferred_element_type=jnp.float32
        ).astype(jnp.bfloat16)
    unsorted = lax.dot_general(
        order_ref[...],
        attended[...],
        (((0,), (0,)), ((), ())),
        preferred_element_type=jnp.float32,
    )
    out_ref[...] = unsorted.astype(jnp.bfloat16).reshape(out_ref.shape)


def pack(query_nope, query_rope, prompt_latent, prompt_rope, response_latent, response_rope, groups):
    bf16 = jnp.bfloat16
    width = query_nope.shape[1] + query_rope.shape[1]
    keys = prompt_latent.shape[0] + prompt_rope.shape[0]
    return pl.pallas_call(
        pack_kernel,
        out_shape=[
            jax.ShapeDtypeStruct((keys, prompt_latent.shape[1]), bf16),
            jax.ShapeDtypeStruct((groups, query_nope.shape[0], width // groups), bf16),
            jax.ShapeDtypeStruct((keys, response_latent.shape[1]), bf16),
        ],
        in_specs=[VMEM] * 6,
        out_specs=[VMEM] * 3,
        name="pack",
        cost_estimate=pl.CostEstimate(flops=0, bytes_accessed=4 * MIB, transcendentals=0),
    )(query_nope, query_rope, prompt_latent, prompt_rope, response_latent, response_rope)


def absorb(position, lengths, prompt_of, response_start, queries, absorb_key, rope):
    head_count, nope, latent = absorb_key.shape
    tokens = queries.shape[0]
    tiles = tokens // TILE
    return pl.pallas_call(
        absorb_kernel,
        out_shape=[
            jax.ShapeDtypeStruct((tiles, head_count, TILE, latent + rope), jnp.bfloat16),
            jax.ShapeDtypeStruct((4, tokens, LANES), jnp.int32),
            jax.ShapeDtypeStruct((tokens, tokens), jnp.bfloat16),
            jax.ShapeDtypeStruct((2 * tiles,), jnp.int32),
        ],
        in_specs=[SMEM, SMEM] + [VMEM] * 5,
        out_specs=[VMEM, VMEM, VMEM, SMEM],
        name="absorb",
        cost_estimate=pl.CostEstimate(
            flops=2 * tokens * head_count * nope * latent,
            bytes_accessed=6 * MIB,
            transcendentals=0,
        ),
        compiler_params=pltpu.CompilerParams(vmem_limit_bytes=16 * MIB),
    )(
        position,
        lengths,
        prompt_of.reshape(1, tokens),
        response_start.reshape(1, tokens),
        jnp.broadcast_to(prompt_of[:, None], (tokens, tokens)),
        queries,
        absorb_key,
    )


def state_shapes(tiles, rows, latent):
    f32 = jnp.float32
    return [
        jax.ShapeDtypeStruct((tiles, rows, latent), f32),
        jax.ShapeDtypeStruct((tiles, rows, LANES), f32),
        jax.ShapeDtypeStruct((tiles, rows, LANES), f32),
    ]


def key_scratch(width, columns, rows, copies):
    scores = pltpu.VMEM((columns // SMALL, rows, SMALL), jnp.float32)
    window = pltpu.VMEM((width, columns), jnp.bfloat16)
    return window, scores, scores, pltpu.SemaphoreType.DMA((copies,))


def cost(queries, latent, columns):
    tiles, rows, width = queries.shape
    return pl.CostEstimate(
        flops=2 * tiles * rows * (width + latent) * columns,
        bytes_accessed=4 * MIB,
        transcendentals=tiles * rows * columns,
    )


def attend_own(factor, bounds, limits, queries, response, own, latent):
    tiles, rows, width = queries.shape
    block = own.shape[1]
    return pl.pallas_call(
        lambda *refs: own_kernel(factor, *refs),
        out_shape=state_shapes(tiles, rows, latent),
        in_specs=[SMEM] + [VMEM] * 3 + [ANYWHERE],
        out_specs=[VMEM] * 3,
        scratch_shapes=list(key_scratch(width, block, rows, 1)),
        name="attend_own",
        cost_estimate=cost(queries, latent, block),
        compiler_params=pltpu.CompilerParams(vmem_limit_bytes=16 * MIB),
    )(bounds, limits, queries, response, own)


def attend_near(factor, position, bounds, limits, queries, state, mine, theirs):
    tiles, rows, width = queries.shape
    latent = state[0].shape[2]
    block = mine[0].shape[1]
    return pl.pallas_call(
        lambda *refs: near_kernel(factor, *refs),
        out_shape=state_shapes(tiles, rows, latent),
        in_specs=[SMEM, SMEM] + [VMEM] * 5 + [ANYWHERE] * 4,
        out_specs=[VMEM] * 3,
        scratch_shapes=list(key_scratch(width, 4 * block, rows, 4)),
        input_output_aliases={4: 0},
        name="attend_near",
        cost_estimate=cost(queries, latent, 2 * block),
        compiler_params=pltpu.CompilerParams(vmem_limit_bytes=24 * MIB),
    )(position, bounds, limits, queries, *state, mine[0], theirs[0], mine[1], theirs[1])


def attend_far(factor, position, bounds, limits, queries, state, value, order, mine, theirs):
    head_count, latent, value_width = value.shape
    tiles, rows, width = queries.shape
    block = mine.shape[1]
    f32 = jnp.float32
    window, even, odd, sems = key_scratch(width, 2 * block, rows, 2)
    return pl.pallas_call(
        lambda *refs: far_kernel(factor, *refs),
        out_shape=jax.ShapeDtypeStruct(
            (tiles * TILE // GROUP, GROUP, head_count * value_width), jnp.bfloat16
        ),
        in_specs=[SMEM, SMEM] + [VMEM] * 7 + [ANYWHERE] * 2,
        out_specs=VMEM,
        scratch_shapes=[
            window,
            even,
            odd,
            pltpu.VMEM((tiles, rows, latent), f32),
            pltpu.VMEM((tiles, rows, LANES), f32),
            pltpu.VMEM((tiles, rows, LANES), f32),
            pltpu.VMEM((head_count, tiles * TILE, latent), jnp.bfloat16),
            pltpu.VMEM((tiles * TILE, head_count * value_width), jnp.bfloat16),
            sems,
        ],
        name="attend_far",
        cost_estimate=cost(queries, latent, block),
        compiler_params=pltpu.CompilerParams(vmem_limit_bytes=24 * MIB),
    )(position, bounds, limits, queries, *state, value, order, mine, theirs)


def local(
    query_nope,
    query_rope,
    absorb_key,
    value_absorption_matrix,
    prompt_latent,
    prompt_rope,
    response_latent,
    response_rope,
    prompt_lengths,
    prompt_of,
    response_start,
):
    head_count, nope_width, latent_width = absorb_key.shape
    value_width = value_absorption_matrix.shape[2]
    rope_width = prompt_rope.shape[0]
    block = prompt_latent.shape[1]
    tokens = response_latent.shape[1]
    groups = lax.axis_size("head")
    length = lax.axis_size("seq")
    seq_index = lax.axis_index("seq")
    head_index = lax.axis_index("head")
    per = tokens // groups
    factor = (nope_width + rope_width) ** (-0.5) * math.log2(math.e)

    own, sent, response = pack(
        query_nope, query_rope, prompt_latent, prompt_rope, response_latent, response_rope, groups
    )
    position = jnp.stack(
        [seq_index * tokens, head_index % 2, (seq_index - REACH) * block]
    ).astype(jnp.int32)
    def onward(distance):
        return [
            (i * groups + h, (i + by) * groups + h)
            for i in range(length)
            for h in range(groups)
            for by in (distance * (1 - 2 * (h % 2)),)
            if 0 <= i + by < length
        ]

    swapped = [(h, h ^ 1) for h in range(groups)]

    arrived = lax.all_to_all(sent, "head", split_axis=0, concat_axis=0, tiled=True)
    queries, limits, order, bounds = absorb(
        position,
        prompt_lengths,
        prompt_of,
        response_start,
        arrived.reshape(tokens, head_count * (nope_width + rope_width)),
        absorb_key,
        rope_width,
    )
    queries = queries.reshape(tokens // TILE, head_count * TILE, latent_width + rope_width)

    first = lax.ppermute(own, ("seq", "head"), onward(1))
    second = lax.ppermute(own, ("seq", "head"), onward(2))
    state = attend_own(factor, bounds, limits, queries, response, own, latent_width)
    second, state = lax.optimization_barrier((second, state))
    third = lax.ppermute(second, ("seq", "head"), onward(1))
    near = [first, second]
    swaps = [lax.ppermute(held, "head", swapped) for held in near]
    state = attend_near(factor, position, bounds, limits, queries, state, near, swaps)
    third, state = lax.optimization_barrier((third, state))
    attended = attend_far(
        factor,
        position,
        bounds,
        limits,
        queries,
        state,
        value_absorption_matrix,
        order,
        third,
        lax.ppermute(third, "head", swapped),
    )
    returned = lax.all_to_all(attended, "head", split_axis=0, concat_axis=0, tiled=True)
    return returned.transpose(1, 0, 2).reshape(per, groups * head_count * value_width)


def solution(mesh):
    return jax.shard_map(
        local,
        mesh=mesh,
        in_specs=(
            P(("seq", "head"), None),
            P(("seq", "head"), None),
            P("head", None, None),
            P("head", None, None),
            P(None, "seq"),
            P(None, "seq"),
            P(None, "seq"),
            P(None, "seq"),
            P(),
            P("seq"),
            P("seq"),
        ),
        out_specs=P(("seq", "head"), None),
        check_vma=False,
    )
```

```python
import math

import jax
import jax.numpy as jnp
from jax import lax
from jax.experimental import pallas as pl
from jax.experimental.pallas import tpu as pltpu
from jax.sharding import PartitionSpec as P

PMAX = 2304
REACH = 3
GROUP = 16
TILE = 32
LANES = 128
SMALL = 256
BIG = 3 * SMALL
NEG = -1e30
MIB = 1024 * 1024

VMEM = pl.BlockSpec(memory_space=pltpu.VMEM)
SMEM = pl.BlockSpec(memory_space=pltpu.SMEM)
ANYWHERE = pl.BlockSpec(memory_space=pl.ANY)


def pack_kernel(
    nope_ref,
    rope_ref,
    latent_ref,
    key_rope_ref,
    response_latent_ref,
    response_rope_ref,
    own_ref,
    sent_ref,
    response_ref,
):
    latent = latent_ref.shape[0]
    groups, _, width = sent_ref.shape
    nope = nope_ref.shape[1] // groups
    rope = rope_ref.shape[1] // groups
    own_ref[:latent, :] = latent_ref[...]
    own_ref[latent:, :] = key_rope_ref[...]
    response_ref[:latent, :] = response_latent_ref[...]
    response_ref[latent:, :] = response_rope_ref[...]
    for g in range(groups):
        sent_ref[g, :, :nope] = nope_ref[:, g * nope : (g + 1) * nope]
        sent_ref[g, :, nope:] = rope_ref[:, g * rope : (g + 1) * rope]


def absorb_kernel(
    position_ref,
    lengths_ref,
    prompt_lane_ref,
    start_lane_ref,
    prompt_row_ref,
    queries_ref,
    absorb_ref,
    out_ref,
    limits_ref,
    order_ref,
    bounds_ref,
):
    head_count, nope, latent = absorb_ref.shape
    tokens = queries_ref.shape[0]
    tiles = tokens // TILE
    rope = out_ref.shape[3] - latent
    by_lane = prompt_lane_ref[...]
    by_row = prompt_row_ref[...]
    row = lax.broadcasted_iota(jnp.int32, (tokens, tokens), 0)
    lane = lax.broadcasted_iota(jnp.int32, (tokens, tokens), 1)
    ahead = (by_row < by_lane) | ((by_row == by_lane) & (row < lane))
    rank = jnp.sum(ahead.astype(jnp.int32), axis=0, keepdims=True)
    chosen = row == rank
    order = chosen.astype(jnp.float32).astype(jnp.bfloat16)
    order_ref[...] = order

    low = jnp.zeros_like(by_lane)
    high = jnp.zeros_like(by_lane)
    start = -position_ref[2]
    for p in range(lengths_ref.shape[0]):
        here = by_lane == p
        end = start + lengths_ref[p]
        low = jnp.where(here, start, low)
        high = jnp.where(here, end, high)
        start = end
    for i, values in enumerate(
        (low, high, start_lane_ref[...] - position_ref[0], lane[:1])
    ):
        sorted_values = jnp.sum(jnp.where(chosen, values, 0), axis=1, keepdims=True)
        limits_ref[i] = jnp.broadcast_to(sorted_values, (tokens, LANES))
    for tile in range(tiles):
        own = slice(tile * TILE, (tile + 1) * TILE)
        bounds_ref[2 * tile] = jnp.min(limits_ref[0, own, :1])
        bounds_ref[2 * tile + 1] = jnp.max(limits_ref[1, own, :1])

    queries = jnp.dot(order, queries_ref[...], preferred_element_type=jnp.float32)
    queries = queries.astype(jnp.bfloat16)
    for h in range(head_count):
        part = jnp.dot(
            queries[:, h * nope : (h + 1) * nope],
            absorb_ref[h],
            preferred_element_type=jnp.float32,
        ).astype(jnp.bfloat16)
        out_ref[:, h, :, :latent] = part.reshape(tiles, TILE, latent)
        first = head_count * nope + h * rope
        out_ref[:, h, :, latent:] = queries[:, first : first + rope].reshape(tiles, TILE, rope)


def place(least, most, span):
    base = least // LANES * LANES
    count = (most - base + SMALL - 1) // SMALL
    return jnp.minimum(base, span - count * SMALL), count


def masked(part, factor, allowed):
    rows, columns = part.shape
    shaped = (part * factor).reshape(rows // TILE, TILE, columns)
    return jnp.where(allowed[None], shaped, NEG).reshape(rows, columns)


def loop(first, last, body):
    @pl.loop(first, last)
    def _(i):
        body(i)


def score_chunk(queries, window, at, slot, count, factor, low, high, lane, scores, peak):
    values = jnp.dot(
        queries, window[:, pl.ds(at, count * SMALL)], preferred_element_type=jnp.float32
    )
    largest = peak[...]
    for j in range(count * SMALL // LANES):
        column = lane + (at + j * LANES)
        part = values[:, j * LANES : (j + 1) * LANES]
        part = masked(part, factor, (column >= low) & (column < high))
        first = j * LANES % SMALL
        scores[slot + j * LANES // SMALL, :, first : first + LANES] = part
        largest = jnp.maximum(largest, part)
    peak[...] = largest


def weigh_chunk(scores, window, at, slot, count, latent, peak, sums, total):
    peak = peak[...]
    parts = []
    for j in range(count * SMALL // LANES):
        first = j * LANES % SMALL
        parts.append(
            jnp.exp2(scores[slot + j * LANES // SMALL, :, first : first + LANES] - peak)
        )
    weights = jnp.concatenate([part.astype(jnp.bfloat16) for part in parts], axis=1)
    total[...] += lax.dot_general(
        weights,
        window[:latent, pl.ds(at, count * SMALL)],
        (((1,), (1,)), ((), ())),
        preferred_element_type=jnp.float32,
    )
    added = parts[0]
    for part in parts[1:]:
        added = added + part
    sums[...] += added


def spread_peak(peak):
    peak[...] = jnp.broadcast_to(jnp.max(peak[...], axis=1, keepdims=True), peak.shape)


def fill(window, pairs, sems):
    copies = []
    for i, (keys, at) in enumerate(pairs):
        target = window.at[:, pl.ds(pl.multiple_of(at, LANES), keys.shape[1])]
        copies.append(pltpu.make_async_copy(keys, target, sems.at[i]))
    for copy in copies:
        copy.start()
    return copies


def run_tiles(
    factor, fold, limits_ref, bounds_ref, queries_ref, window, scores, state, wait, begin, skip
):
    total_ref, peak_ref, sums_ref = state
    tiles = queries_ref.shape[0]
    latent = total_ref.shape[2]
    span = window.shape[1]
    lane = lax.broadcasted_iota(jnp.int32, (TILE, LANES), 1)
    places = [
        place(fold(bounds_ref[2 * tile]), fold(bounds_ref[2 * tile + 1]), span)
        for tile in range(tiles)
    ]
    per = BIG // SMALL

    def score(tile, slot, count):
        own = slice(tile * TILE, (tile + 1) * TILE)
        at = pl.multiple_of(places[tile][0] + slot * SMALL, LANES)
        score_chunk(
            queries_ref[tile],
            window,
            at,
            slot,
            count,
            factor,
            fold(limits_ref[0, own]),
            fold(limits_ref[1, own]),
            lane,
            scores[tile % 2],
            peak_ref.at[tile],
        )

    def weigh(tile, slot, count):
        at = pl.multiple_of(places[tile][0] + slot * SMALL, LANES)
        weigh_chunk(
            scores[tile % 2],
            window,
            at,
            slot,
            count,
            latent,
            peak_ref.at[tile],
            sums_ref.at[tile],
            total_ref.at[tile],
        )

    def rest(tile, done, body):
        count = places[tile][1]
        bigs = count // per
        loop(done, bigs, lambda i: body(tile, i * per, per))
        loop(bigs * per, count, lambda i: body(tile, i, 1))

    wait()
    rest(0, 0, score)
    for tile in range(tiles):
        count = places[tile][1]
        if skip:

            @pl.when(count > 0)
            def _():
                begin(tile)

        else:
            begin(tile)
        if tile + 1 < tiles:
            both = jnp.minimum(count, places[tile + 1][1]) // per

            def fused(i):
                weigh(tile, i * per, per)
                score(tile + 1, i * per, per)

            loop(0, both, fused)
            rest(tile + 1, both, score)
            rest(tile, both, weigh)
        else:
            rest(tile, 0, weigh)


def rescale(before, peak, sums, total):
    change = jnp.exp2(before - peak[...])
    sums[...] *= change
    for at in range(0, total.shape[1], LANES):
        total[:, at : at + LANES] *= change


def own_kernel(
    factor,
    bounds_ref,
    limits_ref,
    queries_ref,
    response_ref,
    own_ref,
    total_ref,
    peak_ref,
    sums_ref,
    window,
    scores_even,
    scores_odd,
    sems,
):
    block = own_ref.shape[1]
    tiles, rows, width = queries_ref.shape
    latent = total_ref.shape[2]
    copies = fill(window, [(own_ref, 0)], sems)
    lane = lax.broadcasted_iota(jnp.int32, (TILE, LANES), 1)
    all_rows = queries_ref[...].reshape(tiles * rows, width)
    own_scores = jnp.dot(all_rows, response_ref[...], preferred_element_type=jnp.float32)
    for tile in range(tiles):
        own = slice(tile * TILE, (tile + 1) * TILE)
        causal = (lane >= limits_ref[2, own]) & (lane <= limits_ref[3, own])
        part = masked(own_scores[tile * rows : (tile + 1) * rows], factor, causal)
        sums_ref[tile] = part
        peak_ref[tile] = part

    def begin(tile):
        spread_peak(peak_ref.at[tile])
        weights = jnp.exp2(sums_ref[tile] - peak_ref[tile])
        sums_ref[tile] = weights
        total_ref[tile] = lax.dot_general(
            weights.astype(jnp.bfloat16),
            response_ref[:latent, :],
            (((1,), (1,)), ((), ())),
            preferred_element_type=jnp.float32,
        )

    def wait():
        for copy in copies:
            copy.wait()

    run_tiles(
        factor,
        lambda x: jnp.clip(x - REACH * block, 0, block),
        limits_ref,
        bounds_ref,
        queries_ref,
        window,
        (scores_even, scores_odd),
        (total_ref, peak_ref, sums_ref),
        wait,
        begin,
        False,
    )


def near_kernel(
    factor,
    position_ref,
    bounds_ref,
    limits_ref,
    queries_ref,
    total_in_ref,
    peak_in_ref,
    sums_in_ref,
    mine1_ref,
    theirs1_ref,
    mine2_ref,
    theirs2_ref,
    total_ref,
    peak_ref,
    sums_ref,
    window,
    scores_even,
    scores_odd,
    sems,
):
    block = mine1_ref.shape[1]
    core = position_ref[1]
    copies = fill(
        window,
        [
            (mine1_ref, (1 + core) * block),
            (theirs1_ref, (2 - core) * block),
            (mine2_ref, 3 * core * block),
            (theirs2_ref, (3 - 3 * core) * block),
        ],
        sems,
    )
    total_ref[...] = total_in_ref[...]
    peak_ref[...] = peak_in_ref[...]
    sums_ref[...] = sums_in_ref[...]

    def fold(x):
        return jnp.where(
            x < REACH * block,
            jnp.maximum(x - block, 0),
            jnp.clip(x - 2 * block, 2 * block, 4 * block),
        )

    def begin(tile):
        spread_peak(peak_ref.at[tile])
        rescale(peak_in_ref[tile], peak_ref.at[tile], sums_ref.at[tile], total_ref.at[tile])

    def wait():
        for copy in copies:
            copy.wait()

    run_tiles(
        factor,
        fold,
        limits_ref,
        bounds_ref,
        queries_ref,
        window,
        (scores_even, scores_odd),
        (total_ref, peak_ref, sums_ref),
        wait,
        begin,
        True,
    )


def far_kernel(
    factor,
    position_ref,
    bounds_ref,
    limits_ref,
    queries_ref,
    total_in_ref,
    peak_in_ref,
    sums_in_ref,
    value_ref,
    order_ref,
    mine_ref,
    theirs_ref,
    out_ref,
    window,
    scores_even,
    scores_odd,
    total,
    peak,
    sums,
    latent_out,
    attended,
    sems,
):
    block = mine_ref.shape[1]
    tiles, rows, _ = queries_ref.shape
    head_count, latent, value_width = value_ref.shape
    core = position_ref[1]
    copies = fill(window, [(mine_ref, core * block), (theirs_ref, (1 - core) * block)], sems)
    skipped = (2 * REACH - 1) * block

    def fold(x):
        return jnp.where(x < block, jnp.maximum(x, 0), jnp.maximum(x - skipped, block))

    total[...] = total_in_ref[...]
    peak[...] = peak_in_ref[...]
    sums[...] = sums_in_ref[...]

    def begin(tile):
        spread_peak(peak.at[tile])
        rescale(peak_in_ref[tile], peak.at[tile], sums.at[tile], total.at[tile])

    def wait():
        for copy in copies:
            copy.wait()

    run_tiles(
        factor,
        fold,
        limits_ref,
        bounds_ref,
        queries_ref,
        window,
        (scores_even, scores_odd),
        (total, peak, sums),
        wait,
        begin,
        True,
    )
    for tile in range(tiles):
        own = slice(tile * TILE, (tile + 1) * TILE)
        share = 1.0 / jnp.sum(sums[tile], axis=1, keepdims=True)
        latent_out[:, own, :] = (
            (total[tile] * share).astype(jnp.bfloat16).reshape(head_count, TILE, latent)
        )
    for h in range(head_count):
        attended[:, h * value_width : (h + 1) * value_width] = jnp.dot(
            latent_out[h], value_ref[h], preferred_element_type=jnp.float32
        ).astype(jnp.bfloat16)
    unsorted = lax.dot_general(
        order_ref[...],
        attended[...],
        (((0,), (0,)), ((), ())),
        preferred_element_type=jnp.float32,
    )
    out_ref[...] = unsorted.astype(jnp.bfloat16).reshape(out_ref.shape)


def pack(query_nope, query_rope, prompt_latent, prompt_rope, response_latent, response_rope, groups):
    bf16 = jnp.bfloat16
    width = query_nope.shape[1] + query_rope.shape[1]
    keys = prompt_latent.shape[0] + prompt_rope.shape[0]
    return pl.pallas_call(
        pack_kernel,
        out_shape=[
            jax.ShapeDtypeStruct((keys, prompt_latent.shape[1]), bf16),
            jax.ShapeDtypeStruct((groups, query_nope.shape[0], width // groups), bf16),
            jax.ShapeDtypeStruct((keys, response_latent.shape[1]), bf16),
        ],
        in_specs=[VMEM] * 6,
        out_specs=[VMEM] * 3,
        name="pack",
        cost_estimate=pl.CostEstimate(flops=0, bytes_accessed=4 * MIB, transcendentals=0),
    )(query_nope, query_rope, prompt_latent, prompt_rope, response_latent, response_rope)


def absorb(position, lengths, prompt_of, response_start, queries, absorb_key, rope):
    head_count, nope, latent = absorb_key.shape
    tokens = queries.shape[0]
    tiles = tokens // TILE
    return pl.pallas_call(
        absorb_kernel,
        out_shape=[
            jax.ShapeDtypeStruct((tiles, head_count, TILE, latent + rope), jnp.bfloat16),
            jax.ShapeDtypeStruct((4, tokens, LANES), jnp.int32),
            jax.ShapeDtypeStruct((tokens, tokens), jnp.bfloat16),
            jax.ShapeDtypeStruct((2 * tiles,), jnp.int32),
        ],
        in_specs=[SMEM, SMEM] + [VMEM] * 5,
        out_specs=[VMEM, VMEM, VMEM, SMEM],
        name="absorb",
        cost_estimate=pl.CostEstimate(
            flops=2 * tokens * head_count * nope * latent,
            bytes_accessed=6 * MIB,
            transcendentals=0,
        ),
        compiler_params=pltpu.CompilerParams(vmem_limit_bytes=16 * MIB),
    )(
        position,
        lengths,
        prompt_of.reshape(1, tokens),
        response_start.reshape(1, tokens),
        jnp.broadcast_to(prompt_of[:, None], (tokens, tokens)),
        queries,
        absorb_key,
    )


def state_shapes(tiles, rows, latent):
    f32 = jnp.float32
    return [
        jax.ShapeDtypeStruct((tiles, rows, latent), f32),
        jax.ShapeDtypeStruct((tiles, rows, LANES), f32),
        jax.ShapeDtypeStruct((tiles, rows, LANES), f32),
    ]


def key_scratch(width, columns, rows, copies):
    scores = pltpu.VMEM((columns // SMALL, rows, SMALL), jnp.float32)
    window = pltpu.VMEM((width, columns), jnp.bfloat16)
    return window, scores, scores, pltpu.SemaphoreType.DMA((copies,))


def cost(queries, latent, columns):
    tiles, rows, width = queries.shape
    return pl.CostEstimate(
        flops=2 * tiles * rows * (width + latent) * columns,
        bytes_accessed=4 * MIB,
        transcendentals=tiles * rows * columns,
    )


def attend_own(factor, bounds, limits, queries, response, own, latent):
    tiles, rows, width = queries.shape
    block = own.shape[1]
    return pl.pallas_call(
        lambda *refs: own_kernel(factor, *refs),
        out_shape=state_shapes(tiles, rows, latent),
        in_specs=[SMEM] + [VMEM] * 3 + [ANYWHERE],
        out_specs=[VMEM] * 3,
        scratch_shapes=list(key_scratch(width, block, rows, 1)),
        name="attend_own",
        cost_estimate=cost(queries, latent, block),
        compiler_params=pltpu.CompilerParams(vmem_limit_bytes=16 * MIB),
    )(bounds, limits, queries, response, own)


def attend_near(factor, position, bounds, limits, queries, state, mine, theirs):
    tiles, rows, width = queries.shape
    latent = state[0].shape[2]
    block = mine[0].shape[1]
    return pl.pallas_call(
        lambda *refs: near_kernel(factor, *refs),
        out_shape=state_shapes(tiles, rows, latent),
        in_specs=[SMEM, SMEM] + [VMEM] * 5 + [ANYWHERE] * 4,
        out_specs=[VMEM] * 3,
        scratch_shapes=list(key_scratch(width, 4 * block, rows, 4)),
        input_output_aliases={4: 0},
        name="attend_near",
        cost_estimate=cost(queries, latent, 2 * block),
        compiler_params=pltpu.CompilerParams(vmem_limit_bytes=24 * MIB),
    )(position, bounds, limits, queries, *state, mine[0], theirs[0], mine[1], theirs[1])


def attend_far(factor, position, bounds, limits, queries, state, value, order, mine, theirs):
    head_count, latent, value_width = value.shape
    tiles, rows, width = queries.shape
    block = mine.shape[1]
    f32 = jnp.float32
    window, even, odd, sems = key_scratch(width, 2 * block, rows, 2)
    return pl.pallas_call(
        lambda *refs: far_kernel(factor, *refs),
        out_shape=jax.ShapeDtypeStruct(
            (tiles * TILE // GROUP, GROUP, head_count * value_width), jnp.bfloat16
        ),
        in_specs=[SMEM, SMEM] + [VMEM] * 7 + [ANYWHERE] * 2,
        out_specs=VMEM,
        scratch_shapes=[
            window,
            even,
            odd,
            pltpu.VMEM((tiles, rows, latent), f32),
            pltpu.VMEM((tiles, rows, LANES), f32),
            pltpu.VMEM((tiles, rows, LANES), f32),
            pltpu.VMEM((head_count, tiles * TILE, latent), jnp.bfloat16),
            pltpu.VMEM((tiles * TILE, head_count * value_width), jnp.bfloat16),
            sems,
        ],
        name="attend_far",
        cost_estimate=cost(queries, latent, block),
        compiler_params=pltpu.CompilerParams(vmem_limit_bytes=24 * MIB),
    )(position, bounds, limits, queries, *state, value, order, mine, theirs)


def local(
    query_nope,
    query_rope,
    absorb_key,
    value_absorption_matrix,
    prompt_latent,
    prompt_rope,
    response_latent,
    response_rope,
    prompt_lengths,
    prompt_of,
    response_start,
):
    head_count, nope_width, latent_width = absorb_key.shape
    value_width = value_absorption_matrix.shape[2]
    rope_width = prompt_rope.shape[0]
    block = prompt_latent.shape[1]
    tokens = response_latent.shape[1]
    groups = lax.axis_size("head")
    length = lax.axis_size("seq")
    seq_index = lax.axis_index("seq")
    head_index = lax.axis_index("head")
    per = tokens // groups
    factor = (nope_width + rope_width) ** (-0.5) * math.log2(math.e)

    own, sent, response = pack(
        query_nope, query_rope, prompt_latent, prompt_rope, response_latent, response_rope, groups
    )
    position = jnp.stack(
        [seq_index * tokens, head_index % 2, (seq_index - REACH) * block]
    ).astype(jnp.int32)
    def onward(distance):
        return [
            (i * groups + h, (i + by) * groups + h)
            for i in range(length)
            for h in range(groups)
            for by in (distance * (1 - 2 * (h % 2)),)
            if 0 <= i + by < length
        ]

    swapped = [(h, h ^ 1) for h in range(groups)]

    arrived = lax.all_to_all(sent, "head", split_axis=0, concat_axis=0, tiled=True)
    queries, limits, order, bounds = absorb(
        position,
        prompt_lengths,
        prompt_of,
        response_start,
        arrived.reshape(tokens, head_count * (nope_width + rope_width)),
        absorb_key,
        rope_width,
    )
    queries = queries.reshape(tokens // TILE, head_count * TILE, latent_width + rope_width)

    first = lax.ppermute(own, ("seq", "head"), onward(1))
    second = lax.ppermute(first, ("seq", "head"), onward(1))
    state = attend_own(factor, bounds, limits, queries, response, own, latent_width)
    second, state = lax.optimization_barrier((second, state))
    third = lax.ppermute(second, ("seq", "head"), onward(1))
    near = [first, second]
    swaps = [lax.ppermute(held, "head", swapped) for held in near]
    state = attend_near(factor, position, bounds, limits, queries, state, near, swaps)
    third, state = lax.optimization_barrier((third, state))
    attended = attend_far(
        factor,
        position,
        bounds,
        limits,
        queries,
        state,
        value_absorption_matrix,
        order,
        third,
        lax.ppermute(third, "head", swapped),
    )
    returned = lax.all_to_all(attended, "head", split_axis=0, concat_axis=0, tiled=True)
    return returned.transpose(1, 0, 2).reshape(per, groups * head_count * value_width)


def solution(mesh):
    return jax.shard_map(
        local,
        mesh=mesh,
        in_specs=(
            P(("seq", "head"), None),
            P(("seq", "head"), None),
            P("head", None, None),
            P("head", None, None),
            P(None, "seq"),
            P(None, "seq"),
            P(None, "seq"),
            P(None, "seq"),
            P(),
            P("seq"),
            P("seq"),
        ),
        out_specs=P(("seq", "head"), None),
        check_vma=False,
    )
```

```python
import math

import jax
import jax.numpy as jnp
from jax import lax
from jax.experimental import pallas as pl
from jax.experimental.pallas import tpu as pltpu
from jax.sharding import PartitionSpec as P

PMAX = 2304
REACH = 3
GROUP = 16
TILE = 64
LANES = 128
SMALL = 256
BIG = 3 * SMALL
NEG = -1e30
MIB = 1024 * 1024

VMEM = pl.BlockSpec(memory_space=pltpu.VMEM)
SMEM = pl.BlockSpec(memory_space=pltpu.SMEM)
ANYWHERE = pl.BlockSpec(memory_space=pl.ANY)


def pack_kernel(
    nope_ref,
    rope_ref,
    latent_ref,
    key_rope_ref,
    response_latent_ref,
    response_rope_ref,
    own_ref,
    sent_ref,
    response_ref,
):
    latent = latent_ref.shape[0]
    groups, _, width = sent_ref.shape
    nope = nope_ref.shape[1] // groups
    rope = rope_ref.shape[1] // groups
    own_ref[:latent, :] = latent_ref[...]
    own_ref[latent:, :] = key_rope_ref[...]
    response_ref[:latent, :] = response_latent_ref[...]
    response_ref[latent:, :] = response_rope_ref[...]
    for g in range(groups):
        sent_ref[g, :, :nope] = nope_ref[:, g * nope : (g + 1) * nope]
        sent_ref[g, :, nope:] = rope_ref[:, g * rope : (g + 1) * rope]


def absorb_kernel(
    position_ref,
    lengths_ref,
    prompt_lane_ref,
    start_lane_ref,
    prompt_row_ref,
    queries_ref,
    absorb_ref,
    out_ref,
    limits_ref,
    order_ref,
    bounds_ref,
):
    head_count, nope, latent = absorb_ref.shape
    tokens = queries_ref.shape[0]
    tiles = tokens // TILE
    rope = out_ref.shape[3] - latent
    by_lane = prompt_lane_ref[...]
    by_row = prompt_row_ref[...]
    row = lax.broadcasted_iota(jnp.int32, (tokens, tokens), 0)
    lane = lax.broadcasted_iota(jnp.int32, (tokens, tokens), 1)
    ahead = (by_row < by_lane) | ((by_row == by_lane) & (row < lane))
    rank = jnp.sum(ahead.astype(jnp.int32), axis=0, keepdims=True)
    chosen = row == rank
    order = chosen.astype(jnp.float32).astype(jnp.bfloat16)
    order_ref[...] = order

    low = jnp.zeros_like(by_lane)
    high = jnp.zeros_like(by_lane)
    start = -position_ref[2]
    for p in range(lengths_ref.shape[0]):
        here = by_lane == p
        end = start + lengths_ref[p]
        low = jnp.where(here, start, low)
        high = jnp.where(here, end, high)
        start = end
    for i, values in enumerate(
        (low, high, start_lane_ref[...] - position_ref[0], lane[:1])
    ):
        sorted_values = jnp.sum(jnp.where(chosen, values, 0), axis=1, keepdims=True)
        limits_ref[i] = jnp.broadcast_to(sorted_values, (tokens, LANES))
    for tile in range(tiles):
        own = slice(tile * TILE, (tile + 1) * TILE)
        bounds_ref[2 * tile] = jnp.min(limits_ref[0, own, :1])
        bounds_ref[2 * tile + 1] = jnp.max(limits_ref[1, own, :1])

    queries = jnp.dot(order, queries_ref[...], preferred_element_type=jnp.float32)
    queries = queries.astype(jnp.bfloat16)
    for h in range(head_count):
        part = jnp.dot(
            queries[:, h * nope : (h + 1) * nope],
            absorb_ref[h],
            preferred_element_type=jnp.float32,
        ).astype(jnp.bfloat16)
        out_ref[:, h, :, :latent] = part.reshape(tiles, TILE, latent)
        first = head_count * nope + h * rope
        out_ref[:, h, :, latent:] = queries[:, first : first + rope].reshape(tiles, TILE, rope)


def place(least, most, span):
    base = least // LANES * LANES
    count = (most - base + SMALL - 1) // SMALL
    return jnp.minimum(base, span - count * SMALL), count


def masked(part, factor, allowed):
    rows, columns = part.shape
    shaped = (part * factor).reshape(rows // TILE, TILE, columns)
    return jnp.where(allowed[None], shaped, NEG).reshape(rows, columns)


def loop(first, last, body):
    @pl.loop(first, last)
    def _(i):
        body(i)


def score_chunk(queries, window, at, slot, count, factor, low, high, lane, scores, peak):
    values = jnp.dot(
        queries, window[:, pl.ds(at, count * SMALL)], preferred_element_type=jnp.float32
    )
    largest = peak[...]
    for j in range(count * SMALL // LANES):
        column = lane + (at + j * LANES)
        part = values[:, j * LANES : (j + 1) * LANES]
        part = masked(part, factor, (column >= low) & (column < high))
        first = j * LANES % SMALL
        scores[slot + j * LANES // SMALL, :, first : first + LANES] = part
        largest = jnp.maximum(largest, part)
    peak[...] = largest


def weigh_chunk(scores, window, at, slot, count, latent, peak, sums, total):
    peak = peak[...]
    parts = []
    for j in range(count * SMALL // LANES):
        first = j * LANES % SMALL
        parts.append(
            jnp.exp2(scores[slot + j * LANES // SMALL, :, first : first + LANES] - peak)
        )
    weights = jnp.concatenate([part.astype(jnp.bfloat16) for part in parts], axis=1)
    total[...] += lax.dot_general(
        weights,
        window[:latent, pl.ds(at, count * SMALL)],
        (((1,), (1,)), ((), ())),
        preferred_element_type=jnp.float32,
    )
    added = parts[0]
    for part in parts[1:]:
        added = added + part
    sums[...] += added


def spread_peak(peak):
    peak[...] = jnp.broadcast_to(jnp.max(peak[...], axis=1, keepdims=True), peak.shape)


def fill(window, pairs, sems):
    copies = []
    for i, (keys, at) in enumerate(pairs):
        target = window.at[:, pl.ds(pl.multiple_of(at, LANES), keys.shape[1])]
        copies.append(pltpu.make_async_copy(keys, target, sems.at[i]))
    for copy in copies:
        copy.start()
    return copies


def run_tiles(
    factor, fold, limits_ref, bounds_ref, queries_ref, window, scores, state, wait, begin, skip
):
    total_ref, peak_ref, sums_ref = state
    tiles = queries_ref.shape[0]
    latent = total_ref.shape[2]
    span = window.shape[1]
    lane = lax.broadcasted_iota(jnp.int32, (TILE, LANES), 1)
    places = [
        place(fold(bounds_ref[2 * tile]), fold(bounds_ref[2 * tile + 1]), span)
        for tile in range(tiles)
    ]
    per = BIG // SMALL

    def score(tile, slot, count):
        own = slice(tile * TILE, (tile + 1) * TILE)
        at = pl.multiple_of(places[tile][0] + slot * SMALL, LANES)
        score_chunk(
            queries_ref[tile],
            window,
            at,
            slot,
            count,
            factor,
            fold(limits_ref[0, own]),
            fold(limits_ref[1, own]),
            lane,
            scores[tile % 2],
            peak_ref.at[tile],
        )

    def weigh(tile, slot, count):
        at = pl.multiple_of(places[tile][0] + slot * SMALL, LANES)
        weigh_chunk(
            scores[tile % 2],
            window,
            at,
            slot,
            count,
            latent,
            peak_ref.at[tile],
            sums_ref.at[tile],
            total_ref.at[tile],
        )

    def rest(tile, done, body):
        count = places[tile][1]
        bigs = count // per
        loop(done, bigs, lambda i: body(tile, i * per, per))
        loop(bigs * per, count, lambda i: body(tile, i, 1))

    wait()
    rest(0, 0, score)
    for tile in range(tiles):
        count = places[tile][1]
        if skip:

            @pl.when(count > 0)
            def _():
                begin(tile)

        else:
            begin(tile)
        if tile + 1 < tiles:
            both = jnp.minimum(count, places[tile + 1][1]) // per

            def fused(i):
                weigh(tile, i * per, per)
                score(tile + 1, i * per, per)

            loop(0, both, fused)
            rest(tile + 1, both, score)
            rest(tile, both, weigh)
        else:
            rest(tile, 0, weigh)


def rescale(before, peak, sums, total):
    change = jnp.exp2(before - peak[...])
    sums[...] *= change
    for at in range(0, total.shape[1], LANES):
        total[:, at : at + LANES] *= change


def own_kernel(
    factor,
    bounds_ref,
    limits_ref,
    queries_ref,
    response_ref,
    own_ref,
    total_ref,
    peak_ref,
    sums_ref,
    window,
    scores_even,
    scores_odd,
    sems,
):
    block = own_ref.shape[1]
    tiles, rows, width = queries_ref.shape
    latent = total_ref.shape[2]
    copies = fill(window, [(own_ref, 0)], sems)
    lane = lax.broadcasted_iota(jnp.int32, (TILE, LANES), 1)
    all_rows = queries_ref[...].reshape(tiles * rows, width)
    own_scores = jnp.dot(all_rows, response_ref[...], preferred_element_type=jnp.float32)
    for tile in range(tiles):
        own = slice(tile * TILE, (tile + 1) * TILE)
        causal = (lane >= limits_ref[2, own]) & (lane <= limits_ref[3, own])
        part = masked(own_scores[tile * rows : (tile + 1) * rows], factor, causal)
        sums_ref[tile] = part
        peak_ref[tile] = part

    def begin(tile):
        spread_peak(peak_ref.at[tile])
        weights = jnp.exp2(sums_ref[tile] - peak_ref[tile])
        sums_ref[tile] = weights
        total_ref[tile] = lax.dot_general(
            weights.astype(jnp.bfloat16),
            response_ref[:latent, :],
            (((1,), (1,)), ((), ())),
            preferred_element_type=jnp.float32,
        )

    def wait():
        for copy in copies:
            copy.wait()

    run_tiles(
        factor,
        lambda x: jnp.clip(x - REACH * block, 0, block),
        limits_ref,
        bounds_ref,
        queries_ref,
        window,
        (scores_even, scores_odd),
        (total_ref, peak_ref, sums_ref),
        wait,
        begin,
        False,
    )


def near_kernel(
    factor,
    position_ref,
    bounds_ref,
    limits_ref,
    queries_ref,
    total_in_ref,
    peak_in_ref,
    sums_in_ref,
    mine1_ref,
    theirs1_ref,
    mine2_ref,
    theirs2_ref,
    total_ref,
    peak_ref,
    sums_ref,
    window,
    scores_even,
    scores_odd,
    sems,
):
    block = mine1_ref.shape[1]
    core = position_ref[1]
    copies = fill(
        window,
        [
            (mine1_ref, (1 + core) * block),
            (theirs1_ref, (2 - core) * block),
            (mine2_ref, 3 * core * block),
            (theirs2_ref, (3 - 3 * core) * block),
        ],
        sems,
    )
    total_ref[...] = total_in_ref[...]
    peak_ref[...] = peak_in_ref[...]
    sums_ref[...] = sums_in_ref[...]

    def fold(x):
        return jnp.where(
            x < REACH * block,
            jnp.maximum(x - block, 0),
            jnp.clip(x - 2 * block, 2 * block, 4 * block),
        )

    def begin(tile):
        spread_peak(peak_ref.at[tile])
        rescale(peak_in_ref[tile], peak_ref.at[tile], sums_ref.at[tile], total_ref.at[tile])

    def wait():
        for copy in copies:
            copy.wait()

    run_tiles(
        factor,
        fold,
        limits_ref,
        bounds_ref,
        queries_ref,
        window,
        (scores_even, scores_odd),
        (total_ref, peak_ref, sums_ref),
        wait,
        begin,
        True,
    )


def far_kernel(
    factor,
    position_ref,
    bounds_ref,
    limits_ref,
    queries_ref,
    total_in_ref,
    peak_in_ref,
    sums_in_ref,
    value_ref,
    order_ref,
    mine_ref,
    theirs_ref,
    out_ref,
    window,
    scores_even,
    scores_odd,
    total,
    peak,
    sums,
    latent_out,
    attended,
    sems,
):
    block = mine_ref.shape[1]
    tiles, rows, _ = queries_ref.shape
    head_count, latent, value_width = value_ref.shape
    core = position_ref[1]
    copies = fill(window, [(mine_ref, core * block), (theirs_ref, (1 - core) * block)], sems)
    skipped = (2 * REACH - 1) * block

    def fold(x):
        return jnp.where(x < block, jnp.maximum(x, 0), jnp.maximum(x - skipped, block))

    total[...] = total_in_ref[...]
    peak[...] = peak_in_ref[...]
    sums[...] = sums_in_ref[...]

    def begin(tile):
        spread_peak(peak.at[tile])
        rescale(peak_in_ref[tile], peak.at[tile], sums.at[tile], total.at[tile])

    def wait():
        for copy in copies:
            copy.wait()

    run_tiles(
        factor,
        fold,
        limits_ref,
        bounds_ref,
        queries_ref,
        window,
        (scores_even, scores_odd),
        (total, peak, sums),
        wait,
        begin,
        True,
    )
    for tile in range(tiles):
        own = slice(tile * TILE, (tile + 1) * TILE)
        share = 1.0 / jnp.sum(sums[tile], axis=1, keepdims=True)
        latent_out[:, own, :] = (
            (total[tile] * share).astype(jnp.bfloat16).reshape(head_count, TILE, latent)
        )
    for h in range(head_count):
        attended[:, h * value_width : (h + 1) * value_width] = jnp.dot(
            latent_out[h], value_ref[h], preferred_element_type=jnp.float32
        ).astype(jnp.bfloat16)
    unsorted = lax.dot_general(
        order_ref[...],
        attended[...],
        (((0,), (0,)), ((), ())),
        preferred_element_type=jnp.float32,
    )
    out_ref[...] = unsorted.astype(jnp.bfloat16).reshape(out_ref.shape)


def pack(query_nope, query_rope, prompt_latent, prompt_rope, response_latent, response_rope, groups):
    bf16 = jnp.bfloat16
    width = query_nope.shape[1] + query_rope.shape[1]
    keys = prompt_latent.shape[0] + prompt_rope.shape[0]
    return pl.pallas_call(
        pack_kernel,
        out_shape=[
            jax.ShapeDtypeStruct((keys, prompt_latent.shape[1]), bf16),
            jax.ShapeDtypeStruct((groups, query_nope.shape[0], width // groups), bf16),
            jax.ShapeDtypeStruct((keys, response_latent.shape[1]), bf16),
        ],
        in_specs=[VMEM] * 6,
        out_specs=[VMEM] * 3,
        name="pack",
        cost_estimate=pl.CostEstimate(flops=0, bytes_accessed=4 * MIB, transcendentals=0),
    )(query_nope, query_rope, prompt_latent, prompt_rope, response_latent, response_rope)


def absorb(position, lengths, prompt_of, response_start, queries, absorb_key, rope):
    head_count, nope, latent = absorb_key.shape
    tokens = queries.shape[0]
    tiles = tokens // TILE
    return pl.pallas_call(
        absorb_kernel,
        out_shape=[
            jax.ShapeDtypeStruct((tiles, head_count, TILE, latent + rope), jnp.bfloat16),
            jax.ShapeDtypeStruct((4, tokens, LANES), jnp.int32),
            jax.ShapeDtypeStruct((tokens, tokens), jnp.bfloat16),
            jax.ShapeDtypeStruct((2 * tiles,), jnp.int32),
        ],
        in_specs=[SMEM, SMEM] + [VMEM] * 5,
        out_specs=[VMEM, VMEM, VMEM, SMEM],
        name="absorb",
        cost_estimate=pl.CostEstimate(
            flops=2 * tokens * head_count * nope * latent,
            bytes_accessed=6 * MIB,
            transcendentals=0,
        ),
        compiler_params=pltpu.CompilerParams(vmem_limit_bytes=16 * MIB),
    )(
        position,
        lengths,
        prompt_of.reshape(1, tokens),
        response_start.reshape(1, tokens),
        jnp.broadcast_to(prompt_of[:, None], (tokens, tokens)),
        queries,
        absorb_key,
    )


def state_shapes(tiles, rows, latent):
    f32 = jnp.float32
    return [
        jax.ShapeDtypeStruct((tiles, rows, latent), f32),
        jax.ShapeDtypeStruct((tiles, rows, LANES), f32),
        jax.ShapeDtypeStruct((tiles, rows, LANES), f32),
    ]


def key_scratch(width, columns, rows, copies):
    scores = pltpu.VMEM((columns // SMALL, rows, SMALL), jnp.float32)
    window = pltpu.VMEM((width, columns), jnp.bfloat16)
    return window, scores, scores, pltpu.SemaphoreType.DMA((copies,))


def cost(queries, latent, columns):
    tiles, rows, width = queries.shape
    return pl.CostEstimate(
        flops=2 * tiles * rows * (width + latent) * columns,
        bytes_accessed=4 * MIB,
        transcendentals=tiles * rows * columns,
    )


def attend_own(factor, bounds, limits, queries, response, own, latent):
    tiles, rows, width = queries.shape
    block = own.shape[1]
    return pl.pallas_call(
        lambda *refs: own_kernel(factor, *refs),
        out_shape=state_shapes(tiles, rows, latent),
        in_specs=[SMEM] + [VMEM] * 3 + [ANYWHERE],
        out_specs=[VMEM] * 3,
        scratch_shapes=list(key_scratch(width, block, rows, 1)),
        name="attend_own",
        cost_estimate=cost(queries, latent, block),
        compiler_params=pltpu.CompilerParams(vmem_limit_bytes=16 * MIB),
    )(bounds, limits, queries, response, own)


def attend_near(factor, position, bounds, limits, queries, state, mine, theirs):
    tiles, rows, width = queries.shape
    latent = state[0].shape[2]
    block = mine[0].shape[1]
    return pl.pallas_call(
        lambda *refs: near_kernel(factor, *refs),
        out_shape=state_shapes(tiles, rows, latent),
        in_specs=[SMEM, SMEM] + [VMEM] * 5 + [ANYWHERE] * 4,
        out_specs=[VMEM] * 3,
        scratch_shapes=list(key_scratch(width, 4 * block, rows, 4)),
        input_output_aliases={4: 0},
        name="attend_near",
        cost_estimate=cost(queries, latent, 2 * block),
        compiler_params=pltpu.CompilerParams(vmem_limit_bytes=36 * MIB),
    )(position, bounds, limits, queries, *state, mine[0], theirs[0], mine[1], theirs[1])


def attend_far(factor, position, bounds, limits, queries, state, value, order, mine, theirs):
    head_count, latent, value_width = value.shape
    tiles, rows, width = queries.shape
    block = mine.shape[1]
    f32 = jnp.float32
    window, even, odd, sems = key_scratch(width, 2 * block, rows, 2)
    return pl.pallas_call(
        lambda *refs: far_kernel(factor, *refs),
        out_shape=jax.ShapeDtypeStruct(
            (tiles * TILE // GROUP, GROUP, head_count * value_width), jnp.bfloat16
        ),
        in_specs=[SMEM, SMEM] + [VMEM] * 7 + [ANYWHERE] * 2,
        out_specs=VMEM,
        scratch_shapes=[
            window,
            even,
            odd,
            pltpu.VMEM((tiles, rows, latent), f32),
            pltpu.VMEM((tiles, rows, LANES), f32),
            pltpu.VMEM((tiles, rows, LANES), f32),
            pltpu.VMEM((head_count, tiles * TILE, latent), jnp.bfloat16),
            pltpu.VMEM((tiles * TILE, head_count * value_width), jnp.bfloat16),
            sems,
        ],
        name="attend_far",
        cost_estimate=cost(queries, latent, block),
        compiler_params=pltpu.CompilerParams(vmem_limit_bytes=30 * MIB),
    )(position, bounds, limits, queries, *state, value, order, mine, theirs)


def local(
    query_nope,
    query_rope,
    absorb_key,
    value_absorption_matrix,
    prompt_latent,
    prompt_rope,
    response_latent,
    response_rope,
    prompt_lengths,
    prompt_of,
    response_start,
):
    head_count, nope_width, latent_width = absorb_key.shape
    value_width = value_absorption_matrix.shape[2]
    rope_width = prompt_rope.shape[0]
    block = prompt_latent.shape[1]
    tokens = response_latent.shape[1]
    groups = lax.axis_size("head")
    length = lax.axis_size("seq")
    seq_index = lax.axis_index("seq")
    head_index = lax.axis_index("head")
    per = tokens // groups
    factor = (nope_width + rope_width) ** (-0.5) * math.log2(math.e)

    own, sent, response = pack(
        query_nope, query_rope, prompt_latent, prompt_rope, response_latent, response_rope, groups
    )
    position = jnp.stack(
        [seq_index * tokens, head_index % 2, (seq_index - REACH) * block]
    ).astype(jnp.int32)
    def onward(distance):
        return [
            (i * groups + h, (i + by) * groups + h)
            for i in range(length)
            for h in range(groups)
            for by in (distance * (1 - 2 * (h % 2)),)
            if 0 <= i + by < length
        ]

    swapped = [(h, h ^ 1) for h in range(groups)]

    arrived = lax.all_to_all(sent, "head", split_axis=0, concat_axis=0, tiled=True)
    queries, limits, order, bounds = absorb(
        position,
        prompt_lengths,
        prompt_of,
        response_start,
        arrived.reshape(tokens, head_count * (nope_width + rope_width)),
        absorb_key,
        rope_width,
    )
    queries = queries.reshape(tokens // TILE, head_count * TILE, latent_width + rope_width)

    first = lax.ppermute(own, ("seq", "head"), onward(1))
    second = lax.ppermute(first, ("seq", "head"), onward(1))
    state = attend_own(factor, bounds, limits, queries, response, own, latent_width)
    second, state = lax.optimization_barrier((second, state))
    third = lax.ppermute(second, ("seq", "head"), onward(1))
    near = [first, second]
    swaps = [lax.ppermute(held, "head", swapped) for held in near]
    state = attend_near(factor, position, bounds, limits, queries, state, near, swaps)
    third, state = lax.optimization_barrier((third, state))
    attended = attend_far(
        factor,
        position,
        bounds,
        limits,
        queries,
        state,
        value_absorption_matrix,
        order,
        third,
        lax.ppermute(third, "head", swapped),
    )
    returned = lax.all_to_all(attended, "head", split_axis=0, concat_axis=0, tiled=True)
    return returned.transpose(1, 0, 2).reshape(per, groups * head_count * value_width)


def solution(mesh):
    return jax.shard_map(
        local,
        mesh=mesh,
        in_specs=(
            P(("seq", "head"), None),
            P(("seq", "head"), None),
            P("head", None, None),
            P("head", None, None),
            P(None, "seq"),
            P(None, "seq"),
            P(None, "seq"),
            P(None, "seq"),
            P(),
            P("seq"),
            P("seq"),
        ),
        out_specs=P(("seq", "head"), None),
        check_vma=False,
    )
```

```python
import math

import jax
import jax.numpy as jnp
from jax import lax
from jax.experimental import pallas as pl
from jax.experimental.pallas import tpu as pltpu
from jax.sharding import PartitionSpec as P

PMAX = 2304
REACH = 3
GROUP = 16
TILE = 64
LANES = 128
SMALL = 256
BIG = 3 * SMALL
NEG = -1e30
MIB = 1024 * 1024

VMEM = pl.BlockSpec(memory_space=pltpu.VMEM)
SMEM = pl.BlockSpec(memory_space=pltpu.SMEM)
ANYWHERE = pl.BlockSpec(memory_space=pl.ANY)


def pack_keys_kernel(latent_ref, rope_ref, response_latent_ref, response_rope_ref, own_ref, response_ref):
    latent = latent_ref.shape[0]
    own_ref[:latent, :] = latent_ref[...]
    own_ref[latent:, :] = rope_ref[...]
    response_ref[:latent, :] = response_latent_ref[...]
    response_ref[latent:, :] = response_rope_ref[...]


def pack_queries_kernel(nope_ref, rope_ref, sent_ref):
    groups = sent_ref.shape[0]
    nope = nope_ref.shape[1] // groups
    rope = rope_ref.shape[1] // groups
    for g in range(groups):
        sent_ref[g, :, :nope] = nope_ref[:, g * nope : (g + 1) * nope]
        sent_ref[g, :, nope:] = rope_ref[:, g * rope : (g + 1) * rope]


def plan_kernel(
    position_ref,
    lengths_ref,
    prompt_lane_ref,
    start_lane_ref,
    prompt_row_ref,
    limits_ref,
    order_ref,
    bounds_ref,
):
    by_lane = prompt_lane_ref[...]
    by_row = prompt_row_ref[...]
    tokens = by_row.shape[0]
    row = lax.broadcasted_iota(jnp.int32, (tokens, tokens), 0)
    lane = lax.broadcasted_iota(jnp.int32, (tokens, tokens), 1)
    ahead = (by_row < by_lane) | ((by_row == by_lane) & (row < lane))
    rank = jnp.sum(ahead.astype(jnp.int32), axis=0, keepdims=True)
    chosen = row == rank
    order_ref[...] = chosen.astype(jnp.float32).astype(jnp.bfloat16)

    low = jnp.zeros_like(by_lane)
    high = jnp.zeros_like(by_lane)
    start = -position_ref[2]
    for p in range(lengths_ref.shape[0]):
        here = by_lane == p
        end = start + lengths_ref[p]
        low = jnp.where(here, start, low)
        high = jnp.where(here, end, high)
        start = end
    for i, values in enumerate(
        (low, high, start_lane_ref[...] - position_ref[0], lane[:1])
    ):
        sorted_values = jnp.sum(jnp.where(chosen, values, 0), axis=1, keepdims=True)
        limits_ref[i] = jnp.broadcast_to(sorted_values, (tokens, LANES))
    for tile in range(tokens // TILE):
        own = slice(tile * TILE, (tile + 1) * TILE)
        bounds_ref[2 * tile] = jnp.min(limits_ref[0, own, :1])
        bounds_ref[2 * tile + 1] = jnp.max(limits_ref[1, own, :1])


def absorb_kernel(order_ref, queries_ref, absorb_ref, out_ref):
    head_count, nope, latent = absorb_ref.shape
    tiles = queries_ref.shape[0] // TILE
    rope = out_ref.shape[3] - latent
    queries = jnp.dot(order_ref[...], queries_ref[...], preferred_element_type=jnp.float32)
    queries = queries.astype(jnp.bfloat16)
    for h in range(head_count):
        part = jnp.dot(
            queries[:, h * nope : (h + 1) * nope],
            absorb_ref[h],
            preferred_element_type=jnp.float32,
        ).astype(jnp.bfloat16)
        out_ref[:, h, :, :latent] = part.reshape(tiles, TILE, latent)
        first = head_count * nope + h * rope
        out_ref[:, h, :, latent:] = queries[:, first : first + rope].reshape(tiles, TILE, rope)


def place(least, most, span):
    base = least // LANES * LANES
    count = (most - base + SMALL - 1) // SMALL
    return jnp.minimum(base, span - count * SMALL), count


def masked(part, factor, allowed):
    rows, columns = part.shape
    shaped = (part * factor).reshape(rows // TILE, TILE, columns)
    return jnp.where(allowed[None], shaped, NEG).reshape(rows, columns)


def loop(first, last, body):
    @pl.loop(first, last)
    def _(i):
        body(i)


def score_chunk(queries, window, at, slot, count, factor, low, high, lane, scores, peak):
    values = jnp.dot(
        queries, window[:, pl.ds(at, count * SMALL)], preferred_element_type=jnp.float32
    )
    largest = peak[...]
    for j in range(count * SMALL // LANES):
        column = lane + (at + j * LANES)
        part = values[:, j * LANES : (j + 1) * LANES]
        part = masked(part, factor, (column >= low) & (column < high))
        first = j * LANES % SMALL
        scores[slot + j * LANES // SMALL, :, first : first + LANES] = part
        largest = jnp.maximum(largest, part)
    peak[...] = largest


def weigh_chunk(scores, window, at, slot, count, latent, peak, sums, total):
    peak = peak[...]
    parts = []
    for j in range(count * SMALL // LANES):
        first = j * LANES % SMALL
        parts.append(
            jnp.exp2(scores[slot + j * LANES // SMALL, :, first : first + LANES] - peak)
        )
    weights = jnp.concatenate([part.astype(jnp.bfloat16) for part in parts], axis=1)
    total[...] += lax.dot_general(
        weights,
        window[:latent, pl.ds(at, count * SMALL)],
        (((1,), (1,)), ((), ())),
        preferred_element_type=jnp.float32,
    )
    added = parts[0]
    for part in parts[1:]:
        added = added + part
    sums[...] += added


def spread_peak(peak):
    peak[...] = jnp.broadcast_to(jnp.max(peak[...], axis=1, keepdims=True), peak.shape)


def fill(window, pairs, sems):
    copies = []
    for i, (keys, at) in enumerate(pairs):
        target = window.at[:, pl.ds(pl.multiple_of(at, LANES), keys.shape[1])]
        copies.append(pltpu.make_async_copy(keys, target, sems.at[i]))
    for copy in copies:
        copy.start()
    return copies


def run_tiles(
    factor, fold, limits_ref, bounds_ref, queries_ref, window, scores, state, wait, begin, skip
):
    total_ref, peak_ref, sums_ref = state
    tiles = queries_ref.shape[0]
    latent = total_ref.shape[2]
    span = window.shape[1]
    lane = lax.broadcasted_iota(jnp.int32, (TILE, LANES), 1)
    places = [
        place(fold(bounds_ref[2 * tile]), fold(bounds_ref[2 * tile + 1]), span)
        for tile in range(tiles)
    ]
    per = BIG // SMALL

    def score(tile, slot, count):
        own = slice(tile * TILE, (tile + 1) * TILE)
        at = pl.multiple_of(places[tile][0] + slot * SMALL, LANES)
        score_chunk(
            queries_ref[tile],
            window,
            at,
            slot,
            count,
            factor,
            fold(limits_ref[0, own]),
            fold(limits_ref[1, own]),
            lane,
            scores[tile % 2],
            peak_ref.at[tile],
        )

    def weigh(tile, slot, count):
        at = pl.multiple_of(places[tile][0] + slot * SMALL, LANES)
        weigh_chunk(
            scores[tile % 2],
            window,
            at,
            slot,
            count,
            latent,
            peak_ref.at[tile],
            sums_ref.at[tile],
            total_ref.at[tile],
        )

    def rest(tile, done, body):
        count = places[tile][1]
        bigs = count // per
        loop(done, bigs, lambda i: body(tile, i * per, per))
        loop(bigs * per, count, lambda i: body(tile, i, 1))

    wait()
    rest(0, 0, score)
    for tile in range(tiles):
        count = places[tile][1]
        if skip is None:
            begin(tile)
        else:

            @pl.when(count > 0)
            def _():
                begin(tile)

            @pl.when(count == 0)
            def _():
                skip(tile)

        if tile + 1 < tiles:
            both = jnp.minimum(count, places[tile + 1][1]) // per

            def fused(i):
                weigh(tile, i * per, per)
                score(tile + 1, i * per, per)

            loop(0, both, fused)
            rest(tile + 1, both, score)
            rest(tile, both, weigh)
        else:
            rest(tile, 0, weigh)


def rescale(before, peak, state):
    change = jnp.exp2(before - peak[...])
    (total_in, total), (sums_in, sums) = state
    sums[...] = sums_in[...] * change
    for at in range(0, total.shape[1], LANES):
        total[:, at : at + LANES] = total_in[:, at : at + LANES] * change


def own_kernel(
    factor,
    bounds_ref,
    limits_ref,
    queries_ref,
    response_ref,
    own_ref,
    total_ref,
    peak_ref,
    sums_ref,
    window,
    scores_even,
    scores_odd,
    sems,
):
    block = own_ref.shape[1]
    tiles, rows, width = queries_ref.shape
    latent = total_ref.shape[2]
    copies = fill(window, [(own_ref, 0)], sems)
    lane = lax.broadcasted_iota(jnp.int32, (TILE, LANES), 1)
    all_rows = queries_ref[...].reshape(tiles * rows, width)
    own_scores = jnp.dot(all_rows, response_ref[...], preferred_element_type=jnp.float32)
    for tile in range(tiles):
        own = slice(tile * TILE, (tile + 1) * TILE)
        causal = (lane >= limits_ref[2, own]) & (lane <= limits_ref[3, own])
        part = masked(own_scores[tile * rows : (tile + 1) * rows], factor, causal)
        sums_ref[tile] = part
        peak_ref[tile] = part

    def begin(tile):
        spread_peak(peak_ref.at[tile])
        weights = jnp.exp2(sums_ref[tile] - peak_ref[tile])
        sums_ref[tile] = weights
        total_ref[tile] = lax.dot_general(
            weights.astype(jnp.bfloat16),
            response_ref[:latent, :],
            (((1,), (1,)), ((), ())),
            preferred_element_type=jnp.float32,
        )

    def wait():
        for copy in copies:
            copy.wait()

    run_tiles(
        factor,
        lambda x: jnp.clip(x - REACH * block, 0, block),
        limits_ref,
        bounds_ref,
        queries_ref,
        window,
        (scores_even, scores_odd),
        (total_ref, peak_ref, sums_ref),
        wait,
        begin,
        None,
    )


def near_kernel(
    factor,
    position_ref,
    bounds_ref,
    limits_ref,
    queries_ref,
    total_in_ref,
    peak_in_ref,
    sums_in_ref,
    mine1_ref,
    theirs1_ref,
    mine2_ref,
    theirs2_ref,
    total_ref,
    peak_ref,
    sums_ref,
    window,
    scores_even,
    scores_odd,
    sems,
):
    block = mine1_ref.shape[1]
    core = position_ref[1]
    copies = fill(
        window,
        [
            (mine1_ref, (1 + core) * block),
            (theirs1_ref, (2 - core) * block),
            (mine2_ref, 3 * core * block),
            (theirs2_ref, (3 - 3 * core) * block),
        ],
        sems,
    )
    peak_ref[...] = peak_in_ref[...]

    def fold(x):
        return jnp.where(
            x < REACH * block,
            jnp.maximum(x - block, 0),
            jnp.clip(x - 2 * block, 2 * block, 4 * block),
        )

    def begin(tile):
        spread_peak(peak_ref.at[tile])
        pairs = (total_in_ref.at[tile], total_ref.at[tile]), (sums_in_ref.at[tile], sums_ref.at[tile])
        rescale(peak_in_ref[tile], peak_ref.at[tile], pairs)

    def skip(tile):
        total_ref[tile] = total_in_ref[tile]
        sums_ref[tile] = sums_in_ref[tile]

    def wait():
        for copy in copies:
            copy.wait()

    run_tiles(
        factor,
        fold,
        limits_ref,
        bounds_ref,
        queries_ref,
        window,
        (scores_even, scores_odd),
        (total_ref, peak_ref, sums_ref),
        wait,
        begin,
        skip,
    )


def far_kernel(
    factor,
    position_ref,
    bounds_ref,
    limits_ref,
    queries_ref,
    total_in_ref,
    peak_in_ref,
    sums_in_ref,
    value_ref,
    order_ref,
    mine_ref,
    theirs_ref,
    out_ref,
    window,
    scores_even,
    scores_odd,
    total,
    peak,
    sums,
    latent_out,
    attended,
    sems,
):
    block = mine_ref.shape[1]
    tiles, rows, _ = queries_ref.shape
    head_count, latent, value_width = value_ref.shape
    core = position_ref[1]
    copies = fill(window, [(mine_ref, core * block), (theirs_ref, (1 - core) * block)], sems)
    skipped = (2 * REACH - 1) * block

    def fold(x):
        return jnp.where(x < block, jnp.maximum(x, 0), jnp.maximum(x - skipped, block))

    peak[...] = peak_in_ref[...]

    def begin(tile):
        spread_peak(peak.at[tile])
        pairs = (total_in_ref.at[tile], total.at[tile]), (sums_in_ref.at[tile], sums.at[tile])
        rescale(peak_in_ref[tile], peak.at[tile], pairs)

    def skip(tile):
        total[tile] = total_in_ref[tile]
        sums[tile] = sums_in_ref[tile]

    def wait():
        for copy in copies:
            copy.wait()

    run_tiles(
        factor,
        fold,
        limits_ref,
        bounds_ref,
        queries_ref,
        window,
        (scores_even, scores_odd),
        (total, peak, sums),
        wait,
        begin,
        skip,
    )
    for tile in range(tiles):
        own = slice(tile * TILE, (tile + 1) * TILE)
        share = 1.0 / jnp.sum(sums[tile], axis=1, keepdims=True)
        latent_out[:, own, :] = (
            (total[tile] * share).astype(jnp.bfloat16).reshape(head_count, TILE, latent)
        )
    for h in range(head_count):
        attended[:, h * value_width : (h + 1) * value_width] = jnp.dot(
            latent_out[h], value_ref[h], preferred_element_type=jnp.float32
        ).astype(jnp.bfloat16)
    unsorted = lax.dot_general(
        order_ref[...],
        attended[...],
        (((0,), (0,)), ((), ())),
        preferred_element_type=jnp.float32,
    )
    out_ref[...] = unsorted.astype(jnp.bfloat16).reshape(out_ref.shape)


def pack_keys(prompt_latent, prompt_rope, response_latent, response_rope):
    keys = prompt_latent.shape[0] + prompt_rope.shape[0]
    return pl.pallas_call(
        pack_keys_kernel,
        out_shape=[
            jax.ShapeDtypeStruct((keys, prompt_latent.shape[1]), jnp.bfloat16),
            jax.ShapeDtypeStruct((keys, response_latent.shape[1]), jnp.bfloat16),
        ],
        in_specs=[VMEM] * 4,
        out_specs=[VMEM] * 2,
        name="pack_keys",
        cost_estimate=pl.CostEstimate(flops=0, bytes_accessed=2 * MIB, transcendentals=0),
    )(prompt_latent, prompt_rope, response_latent, response_rope)


def pack_queries(query_nope, query_rope, groups):
    width = query_nope.shape[1] + query_rope.shape[1]
    return pl.pallas_call(
        pack_queries_kernel,
        out_shape=jax.ShapeDtypeStruct((groups, query_nope.shape[0], width // groups), jnp.bfloat16),
        in_specs=[VMEM] * 2,
        out_specs=VMEM,
        name="pack_queries",
        cost_estimate=pl.CostEstimate(flops=0, bytes_accessed=2 * MIB, transcendentals=0),
    )(query_nope, query_rope)


def plan(position, lengths, prompt_of, response_start):
    tokens = prompt_of.shape[0]
    return pl.pallas_call(
        plan_kernel,
        out_shape=[
            jax.ShapeDtypeStruct((4, tokens, LANES), jnp.int32),
            jax.ShapeDtypeStruct((tokens, tokens), jnp.bfloat16),
            jax.ShapeDtypeStruct((2 * tokens // TILE,), jnp.int32),
        ],
        in_specs=[SMEM, SMEM] + [VMEM] * 3,
        out_specs=[VMEM, VMEM, SMEM],
        name="plan",
        cost_estimate=pl.CostEstimate(flops=0, bytes_accessed=2 * MIB, transcendentals=0),
    )(
        position,
        lengths,
        prompt_of.reshape(1, tokens),
        response_start.reshape(1, tokens),
        jnp.broadcast_to(prompt_of[:, None], (tokens, tokens)),
    )


def absorb(order, queries, absorb_key, rope):
    head_count, nope, latent = absorb_key.shape
    tokens = queries.shape[0]
    return pl.pallas_call(
        absorb_kernel,
        out_shape=jax.ShapeDtypeStruct(
            (tokens // TILE, head_count, TILE, latent + rope), jnp.bfloat16
        ),
        in_specs=[VMEM] * 3,
        out_specs=VMEM,
        name="absorb",
        cost_estimate=pl.CostEstimate(
            flops=2 * tokens * head_count * nope * latent,
            bytes_accessed=6 * MIB,
            transcendentals=0,
        ),
        compiler_params=pltpu.CompilerParams(vmem_limit_bytes=16 * MIB),
    )(order, queries, absorb_key)


def state_shapes(tiles, rows, latent):
    f32 = jnp.float32
    return [
        jax.ShapeDtypeStruct((tiles, rows, latent), f32),
        jax.ShapeDtypeStruct((tiles, rows, LANES), f32),
        jax.ShapeDtypeStruct((tiles, rows, LANES), f32),
    ]


def key_scratch(width, columns, rows, copies):
    scores = pltpu.VMEM((columns // SMALL, rows, SMALL), jnp.float32)
    window = pltpu.VMEM((width, columns), jnp.bfloat16)
    return window, scores, scores, pltpu.SemaphoreType.DMA((copies,))


def cost(queries, latent, columns):
    tiles, rows, width = queries.shape
    return pl.CostEstimate(
        flops=2 * tiles * rows * (width + latent) * columns,
        bytes_accessed=4 * MIB,
        transcendentals=tiles * rows * columns,
    )


def attend_own(factor, bounds, limits, queries, response, own, latent):
    tiles, rows, width = queries.shape
    block = own.shape[1]
    return pl.pallas_call(
        lambda *refs: own_kernel(factor, *refs),
        out_shape=state_shapes(tiles, rows, latent),
        in_specs=[SMEM] + [VMEM] * 3 + [ANYWHERE],
        out_specs=[VMEM] * 3,
        scratch_shapes=list(key_scratch(width, block, rows, 1)),
        name="attend_own",
        cost_estimate=cost(queries, latent, block),
        compiler_params=pltpu.CompilerParams(vmem_limit_bytes=16 * MIB),
    )(bounds, limits, queries, response, own)


def attend_near(factor, position, bounds, limits, queries, state, mine, theirs):
    tiles, rows, width = queries.shape
    latent = state[0].shape[2]
    block = mine[0].shape[1]
    return pl.pallas_call(
        lambda *refs: near_kernel(factor, *refs),
        out_shape=state_shapes(tiles, rows, latent),
        in_specs=[SMEM, SMEM] + [VMEM] * 5 + [ANYWHERE] * 4,
        out_specs=[VMEM] * 3,
        scratch_shapes=list(key_scratch(width, 4 * block, rows, 4)),
        input_output_aliases={4: 0},
        name="attend_near",
        cost_estimate=cost(queries, latent, 2 * block),
        compiler_params=pltpu.CompilerParams(vmem_limit_bytes=36 * MIB),
    )(position, bounds, limits, queries, *state, mine[0], theirs[0], mine[1], theirs[1])


def attend_far(factor, position, bounds, limits, queries, state, value, order, mine, theirs):
    head_count, latent, value_width = value.shape
    tiles, rows, width = queries.shape
    block = mine.shape[1]
    f32 = jnp.float32
    window, even, odd, sems = key_scratch(width, 2 * block, rows, 2)
    return pl.pallas_call(
        lambda *refs: far_kernel(factor, *refs),
        out_shape=jax.ShapeDtypeStruct(
            (tiles * TILE // GROUP, GROUP, head_count * value_width), jnp.bfloat16
        ),
        in_specs=[SMEM, SMEM] + [VMEM] * 7 + [ANYWHERE] * 2,
        out_specs=VMEM,
        scratch_shapes=[
            window,
            even,
            odd,
            pltpu.VMEM((tiles, rows, latent), f32),
            pltpu.VMEM((tiles, rows, LANES), f32),
            pltpu.VMEM((tiles, rows, LANES), f32),
            pltpu.VMEM((head_count, tiles * TILE, latent), jnp.bfloat16),
            pltpu.VMEM((tiles * TILE, head_count * value_width), jnp.bfloat16),
            sems,
        ],
        name="attend_far",
        cost_estimate=cost(queries, latent, block),
        compiler_params=pltpu.CompilerParams(vmem_limit_bytes=30 * MIB),
    )(position, bounds, limits, queries, *state, value, order, mine, theirs)


def local(
    query_nope,
    query_rope,
    absorb_key,
    value_absorption_matrix,
    prompt_latent,
    prompt_rope,
    response_latent,
    response_rope,
    prompt_lengths,
    prompt_of,
    response_start,
):
    head_count, nope_width, latent_width = absorb_key.shape
    value_width = value_absorption_matrix.shape[2]
    rope_width = prompt_rope.shape[0]
    block = prompt_latent.shape[1]
    tokens = response_latent.shape[1]
    groups = lax.axis_size("head")
    length = lax.axis_size("seq")
    seq_index = lax.axis_index("seq")
    head_index = lax.axis_index("head")
    per = tokens // groups
    factor = (nope_width + rope_width) ** (-0.5) * math.log2(math.e)

    own, response = pack_keys(prompt_latent, prompt_rope, response_latent, response_rope)
    sent = pack_queries(query_nope, query_rope, groups)
    position = jnp.stack(
        [seq_index * tokens, head_index % 2, (seq_index - REACH) * block]
    ).astype(jnp.int32)
    def onward(distance):
        return [
            (i * groups + h, (i + by) * groups + h)
            for i in range(length)
            for h in range(groups)
            for by in (distance * (1 - 2 * (h % 2)),)
            if 0 <= i + by < length
        ]

    swapped = [(h, h ^ 1) for h in range(groups)]

    arrived = lax.all_to_all(sent, "head", split_axis=0, concat_axis=0, tiled=True)
    first = lax.ppermute(own, ("seq", "head"), onward(1))
    first, prompt_of = lax.optimization_barrier((first, prompt_of))
    limits, order, bounds = plan(position, prompt_lengths, prompt_of, response_start)
    queries = absorb(
        order,
        arrived.reshape(tokens, head_count * (nope_width + rope_width)),
        absorb_key,
        rope_width,
    )
    queries = queries.reshape(tokens // TILE, head_count * TILE, latent_width + rope_width)

    second = lax.ppermute(first, ("seq", "head"), onward(1))
    state = attend_own(factor, bounds, limits, queries, response, own, latent_width)
    second, state = lax.optimization_barrier((second, state))
    third = lax.ppermute(second, ("seq", "head"), onward(1))
    near = [first, second]
    swaps = [lax.ppermute(held, "head", swapped) for held in near]
    state = attend_near(factor, position, bounds, limits, queries, state, near, swaps)
    third, state = lax.optimization_barrier((third, state))
    attended = attend_far(
        factor,
        position,
        bounds,
        limits,
        queries,
        state,
        value_absorption_matrix,
        order,
        third,
        lax.ppermute(third, "head", swapped),
    )
    returned = lax.all_to_all(attended, "head", split_axis=0, concat_axis=0, tiled=True)
    return returned.transpose(1, 0, 2).reshape(per, groups * head_count * value_width)


def solution(mesh):
    return jax.shard_map(
        local,
        mesh=mesh,
        in_specs=(
            P(("seq", "head"), None),
            P(("seq", "head"), None),
            P("head", None, None),
            P("head", None, None),
            P(None, "seq"),
            P(None, "seq"),
            P(None, "seq"),
            P(None, "seq"),
            P(),
            P("seq"),
            P("seq"),
        ),
        out_specs=P(("seq", "head"), None),
        check_vma=False,
    )
```

```python
import math

import jax
import jax.numpy as jnp
from jax import lax
from jax.experimental import pallas as pl
from jax.experimental.pallas import tpu as pltpu
from jax.sharding import PartitionSpec as P

PMAX = 2304
REACH = 3
GROUP = 16
TILE = 64
LANES = 128
SMALL = 256
BIG = 3 * SMALL
NEG = -1e30
MIB = 1024 * 1024

VMEM = pl.BlockSpec(memory_space=pltpu.VMEM)
SMEM = pl.BlockSpec(memory_space=pltpu.SMEM)
ANYWHERE = pl.BlockSpec(memory_space=pl.ANY)


def pack_kernel(nope_ref, rope_ref, response_latent_ref, response_rope_ref, sent_ref, response_ref):
    latent = response_latent_ref.shape[0]
    groups, _, width = sent_ref.shape
    nope = nope_ref.shape[1] // groups
    rope = rope_ref.shape[1] // groups
    response_ref[:latent, :] = response_latent_ref[...]
    response_ref[latent:, :] = response_rope_ref[...]
    for g in range(groups):
        sent_ref[g, :, :nope] = nope_ref[:, g * nope : (g + 1) * nope]
        sent_ref[g, :, nope:] = rope_ref[:, g * rope : (g + 1) * rope]


def join_kernel(latent_ref, rope_ref, joined_ref):
    latent = latent_ref.shape[0]
    joined_ref[:latent, :] = latent_ref[...]
    joined_ref[latent:, :] = rope_ref[...]


def absorb_kernel(
    position_ref,
    lengths_ref,
    prompt_lane_ref,
    start_lane_ref,
    prompt_row_ref,
    queries_ref,
    absorb_ref,
    out_ref,
    limits_ref,
    order_ref,
    bounds_ref,
):
    head_count, nope, latent = absorb_ref.shape
    tokens = queries_ref.shape[0]
    tiles = tokens // TILE
    rope = out_ref.shape[3] - latent
    by_lane = prompt_lane_ref[...]
    by_row = prompt_row_ref[...]
    row = lax.broadcasted_iota(jnp.int32, (tokens, tokens), 0)
    lane = lax.broadcasted_iota(jnp.int32, (tokens, tokens), 1)
    ahead = (by_row < by_lane) | ((by_row == by_lane) & (row < lane))
    rank = jnp.sum(ahead.astype(jnp.int32), axis=0, keepdims=True)
    chosen = row == rank
    order = chosen.astype(jnp.float32).astype(jnp.bfloat16)
    order_ref[...] = order

    low = jnp.zeros_like(by_lane)
    high = jnp.zeros_like(by_lane)
    start = -position_ref[2]
    for p in range(lengths_ref.shape[0]):
        here = by_lane == p
        end = start + lengths_ref[p]
        low = jnp.where(here, start, low)
        high = jnp.where(here, end, high)
        start = end
    for i, values in enumerate(
        (low, high, start_lane_ref[...] - position_ref[0], lane[:1])
    ):
        sorted_values = jnp.sum(jnp.where(chosen, values, 0), axis=1, keepdims=True)
        limits_ref[i] = jnp.broadcast_to(sorted_values, (tokens, LANES))
    for tile in range(tiles):
        own = slice(tile * TILE, (tile + 1) * TILE)
        bounds_ref[2 * tile] = jnp.min(limits_ref[0, own, :1])
        bounds_ref[2 * tile + 1] = jnp.max(limits_ref[1, own, :1])

    queries = jnp.dot(order, queries_ref[...], preferred_element_type=jnp.float32)
    queries = queries.astype(jnp.bfloat16)
    for h in range(head_count):
        part = jnp.dot(
            queries[:, h * nope : (h + 1) * nope],
            absorb_ref[h],
            preferred_element_type=jnp.float32,
        ).astype(jnp.bfloat16)
        out_ref[:, h, :, :latent] = part.reshape(tiles, TILE, latent)
        first = head_count * nope + h * rope
        out_ref[:, h, :, latent:] = queries[:, first : first + rope].reshape(tiles, TILE, rope)


def place(least, most, span):
    base = least // LANES * LANES
    count = (most - base + SMALL - 1) // SMALL
    return jnp.minimum(base, span - count * SMALL), count


def masked(part, factor, allowed):
    rows, columns = part.shape
    shaped = (part * factor).reshape(rows // TILE, TILE, columns)
    return jnp.where(allowed[None], shaped, NEG).reshape(rows, columns)


def loop(first, last, body):
    @pl.loop(first, last)
    def _(i):
        body(i)


def score_chunk(queries, window, at, slot, count, factor, low, high, lane, scores, peak):
    values = jnp.dot(
        queries, window[:, pl.ds(at, count * SMALL)], preferred_element_type=jnp.float32
    )
    largest = peak[...]
    for j in range(count * SMALL // LANES):
        column = lane + (at + j * LANES)
        part = values[:, j * LANES : (j + 1) * LANES]
        part = masked(part, factor, (column >= low) & (column < high))
        first = j * LANES % SMALL
        scores[slot + j * LANES // SMALL, :, first : first + LANES] = part
        largest = jnp.maximum(largest, part)
    peak[...] = largest


def weigh_chunk(scores, window, at, slot, count, latent, peak, sums, total):
    peak = peak[...]
    parts = []
    for j in range(count * SMALL // LANES):
        first = j * LANES % SMALL
        parts.append(
            jnp.exp2(scores[slot + j * LANES // SMALL, :, first : first + LANES] - peak)
        )
    weights = jnp.concatenate([part.astype(jnp.bfloat16) for part in parts], axis=1)
    total[...] += lax.dot_general(
        weights,
        window[:latent, pl.ds(at, count * SMALL)],
        (((1,), (1,)), ((), ())),
        preferred_element_type=jnp.float32,
    )
    added = parts[0]
    for part in parts[1:]:
        added = added + part
    sums[...] += added


def spread_peak(peak):
    peak[...] = jnp.broadcast_to(jnp.max(peak[...], axis=1, keepdims=True), peak.shape)


def fill(window, pairs, sems):
    copies = []
    for i, (keys, at) in enumerate(pairs):
        target = window.at[:, pl.ds(pl.multiple_of(at, LANES), keys.shape[1])]
        copies.append(pltpu.make_async_copy(keys, target, sems.at[i]))
    for copy in copies:
        copy.start()
    return copies


def run_tiles(
    factor, fold, limits_ref, bounds_ref, queries_ref, window, scores, state, wait, begin, skip
):
    total_ref, peak_ref, sums_ref = state
    tiles = queries_ref.shape[0]
    latent = total_ref.shape[2]
    span = window.shape[1]
    lane = lax.broadcasted_iota(jnp.int32, (TILE, LANES), 1)
    places = [
        place(fold(bounds_ref[2 * tile]), fold(bounds_ref[2 * tile + 1]), span)
        for tile in range(tiles)
    ]
    per = BIG // SMALL

    def score(tile, slot, count):
        own = slice(tile * TILE, (tile + 1) * TILE)
        at = pl.multiple_of(places[tile][0] + slot * SMALL, LANES)
        score_chunk(
            queries_ref[tile],
            window,
            at,
            slot,
            count,
            factor,
            fold(limits_ref[0, own]),
            fold(limits_ref[1, own]),
            lane,
            scores[tile % 2],
            peak_ref.at[tile],
        )

    def weigh(tile, slot, count):
        at = pl.multiple_of(places[tile][0] + slot * SMALL, LANES)
        weigh_chunk(
            scores[tile % 2],
            window,
            at,
            slot,
            count,
            latent,
            peak_ref.at[tile],
            sums_ref.at[tile],
            total_ref.at[tile],
        )

    def rest(tile, done, body):
        count = places[tile][1]
        bigs = count // per
        loop(done, bigs, lambda i: body(tile, i * per, per))
        loop(bigs * per, count, lambda i: body(tile, i, 1))

    wait()
    rest(0, 0, score)
    for tile in range(tiles):
        count = places[tile][1]
        if skip is None:
            begin(tile)
        else:

            @pl.when(count > 0)
            def _():
                begin(tile)

            @pl.when(count == 0)
            def _():
                skip(tile)

        if tile + 1 < tiles:
            both = jnp.minimum(count, places[tile + 1][1]) // per

            def fused(i):
                weigh(tile, i * per, per)
                score(tile + 1, i * per, per)

            loop(0, both, fused)
            rest(tile + 1, both, score)
            rest(tile, both, weigh)
        else:
            rest(tile, 0, weigh)


def rescale(before, peak, state):
    change = jnp.exp2(before - peak[...])
    (total_in, total), (sums_in, sums) = state
    sums[...] = sums_in[...] * change
    for at in range(0, total.shape[1], LANES):
        total[:, at : at + LANES] = total_in[:, at : at + LANES] * change


def own_kernel(
    factor,
    bounds_ref,
    limits_ref,
    queries_ref,
    response_ref,
    latent_ref,
    rope_ref,
    total_ref,
    peak_ref,
    sums_ref,
    window,
    scores_even,
    scores_odd,
    sems,
):
    block = latent_ref.shape[1]
    tiles, rows, width = queries_ref.shape
    latent = total_ref.shape[2]
    copies = [
        pltpu.make_async_copy(latent_ref, window.at[:latent], sems.at[0]),
        pltpu.make_async_copy(rope_ref, window.at[latent:], sems.at[1]),
    ]
    for copy in copies:
        copy.start()
    lane = lax.broadcasted_iota(jnp.int32, (TILE, LANES), 1)
    all_rows = queries_ref[...].reshape(tiles * rows, width)
    own_scores = jnp.dot(all_rows, response_ref[...], preferred_element_type=jnp.float32)
    for tile in range(tiles):
        own = slice(tile * TILE, (tile + 1) * TILE)
        causal = (lane >= limits_ref[2, own]) & (lane <= limits_ref[3, own])
        part = masked(own_scores[tile * rows : (tile + 1) * rows], factor, causal)
        sums_ref[tile] = part
        peak_ref[tile] = part

    def begin(tile):
        spread_peak(peak_ref.at[tile])
        weights = jnp.exp2(sums_ref[tile] - peak_ref[tile])
        sums_ref[tile] = weights
        total_ref[tile] = lax.dot_general(
            weights.astype(jnp.bfloat16),
            response_ref[:latent, :],
            (((1,), (1,)), ((), ())),
            preferred_element_type=jnp.float32,
        )

    def wait():
        for copy in copies:
            copy.wait()

    run_tiles(
        factor,
        lambda x: jnp.clip(x - REACH * block, 0, block),
        limits_ref,
        bounds_ref,
        queries_ref,
        window,
        (scores_even, scores_odd),
        (total_ref, peak_ref, sums_ref),
        wait,
        begin,
        None,
    )


def near_kernel(
    factor,
    position_ref,
    bounds_ref,
    limits_ref,
    queries_ref,
    total_in_ref,
    peak_in_ref,
    sums_in_ref,
    mine1_ref,
    theirs1_ref,
    mine2_ref,
    theirs2_ref,
    total_ref,
    peak_ref,
    sums_ref,
    window,
    scores_even,
    scores_odd,
    sems,
):
    block = mine1_ref.shape[1]
    core = position_ref[1]
    copies = fill(
        window,
        [
            (mine1_ref, (1 + core) * block),
            (theirs1_ref, (2 - core) * block),
            (mine2_ref, 3 * core * block),
            (theirs2_ref, (3 - 3 * core) * block),
        ],
        sems,
    )
    peak_ref[...] = peak_in_ref[...]

    def fold(x):
        return jnp.where(
            x < REACH * block,
            jnp.maximum(x - block, 0),
            jnp.clip(x - 2 * block, 2 * block, 4 * block),
        )

    def begin(tile):
        spread_peak(peak_ref.at[tile])
        pairs = (total_in_ref.at[tile], total_ref.at[tile]), (sums_in_ref.at[tile], sums_ref.at[tile])
        rescale(peak_in_ref[tile], peak_ref.at[tile], pairs)

    def skip(tile):
        total_ref[tile] = total_in_ref[tile]
        sums_ref[tile] = sums_in_ref[tile]

    def wait():
        for copy in copies:
            copy.wait()

    run_tiles(
        factor,
        fold,
        limits_ref,
        bounds_ref,
        queries_ref,
        window,
        (scores_even, scores_odd),
        (total_ref, peak_ref, sums_ref),
        wait,
        begin,
        skip,
    )


def far_kernel(
    factor,
    position_ref,
    bounds_ref,
    limits_ref,
    queries_ref,
    total_in_ref,
    peak_in_ref,
    sums_in_ref,
    value_ref,
    order_ref,
    mine_ref,
    theirs_ref,
    out_ref,
    window,
    scores_even,
    scores_odd,
    total,
    peak,
    sums,
    latent_out,
    attended,
    sems,
):
    block = mine_ref.shape[1]
    tiles, rows, _ = queries_ref.shape
    head_count, latent, value_width = value_ref.shape
    core = position_ref[1]
    copies = fill(window, [(mine_ref, core * block), (theirs_ref, (1 - core) * block)], sems)
    skipped = (2 * REACH - 1) * block

    def fold(x):
        return jnp.where(x < block, jnp.maximum(x, 0), jnp.maximum(x - skipped, block))

    peak[...] = peak_in_ref[...]

    def begin(tile):
        spread_peak(peak.at[tile])
        pairs = (total_in_ref.at[tile], total.at[tile]), (sums_in_ref.at[tile], sums.at[tile])
        rescale(peak_in_ref[tile], peak.at[tile], pairs)

    def skip(tile):
        total[tile] = total_in_ref[tile]
        sums[tile] = sums_in_ref[tile]

    def wait():
        for copy in copies:
            copy.wait()

    run_tiles(
        factor,
        fold,
        limits_ref,
        bounds_ref,
        queries_ref,
        window,
        (scores_even, scores_odd),
        (total, peak, sums),
        wait,
        begin,
        skip,
    )
    for tile in range(tiles):
        own = slice(tile * TILE, (tile + 1) * TILE)
        share = 1.0 / jnp.sum(sums[tile], axis=1, keepdims=True)
        latent_out[:, own, :] = (
            (total[tile] * share).astype(jnp.bfloat16).reshape(head_count, TILE, latent)
        )
    for h in range(head_count):
        attended[:, h * value_width : (h + 1) * value_width] = jnp.dot(
            latent_out[h], value_ref[h], preferred_element_type=jnp.float32
        ).astype(jnp.bfloat16)
    unsorted = lax.dot_general(
        order_ref[...],
        attended[...],
        (((0,), (0,)), ((), ())),
        preferred_element_type=jnp.float32,
    )
    out_ref[...] = unsorted.astype(jnp.bfloat16).reshape(out_ref.shape)


def pack(query_nope, query_rope, response_latent, response_rope, groups):
    bf16 = jnp.bfloat16
    width = query_nope.shape[1] + query_rope.shape[1]
    keys = response_latent.shape[0] + response_rope.shape[0]
    return pl.pallas_call(
        pack_kernel,
        out_shape=[
            jax.ShapeDtypeStruct((groups, query_nope.shape[0], width // groups), bf16),
            jax.ShapeDtypeStruct((keys, response_latent.shape[1]), bf16),
        ],
        in_specs=[VMEM] * 4,
        out_specs=[VMEM] * 2,
        name="pack",
        cost_estimate=pl.CostEstimate(flops=0, bytes_accessed=2 * MIB, transcendentals=0),
    )(query_nope, query_rope, response_latent, response_rope)


def join(latent, rope):
    return pl.pallas_call(
        join_kernel,
        out_shape=jax.ShapeDtypeStruct(
            (latent.shape[0] + rope.shape[0], latent.shape[1]), jnp.bfloat16
        ),
        in_specs=[VMEM] * 2,
        out_specs=VMEM,
        name="join",
        cost_estimate=pl.CostEstimate(flops=0, bytes_accessed=2 * MIB, transcendentals=0),
    )(latent, rope)


def absorb(position, lengths, prompt_of, response_start, queries, absorb_key, rope):
    head_count, nope, latent = absorb_key.shape
    tokens = queries.shape[0]
    tiles = tokens // TILE
    return pl.pallas_call(
        absorb_kernel,
        out_shape=[
            jax.ShapeDtypeStruct((tiles, head_count, TILE, latent + rope), jnp.bfloat16),
            jax.ShapeDtypeStruct((4, tokens, LANES), jnp.int32),
            jax.ShapeDtypeStruct((tokens, tokens), jnp.bfloat16),
            jax.ShapeDtypeStruct((2 * tiles,), jnp.int32),
        ],
        in_specs=[SMEM, SMEM] + [VMEM] * 5,
        out_specs=[VMEM, VMEM, VMEM, SMEM],
        name="absorb",
        cost_estimate=pl.CostEstimate(
            flops=2 * tokens * head_count * nope * latent,
            bytes_accessed=6 * MIB,
            transcendentals=0,
        ),
        compiler_params=pltpu.CompilerParams(vmem_limit_bytes=16 * MIB),
    )(
        position,
        lengths,
        prompt_of.reshape(1, tokens),
        response_start.reshape(1, tokens),
        jnp.broadcast_to(prompt_of[:, None], (tokens, tokens)),
        queries,
        absorb_key,
    )


def state_shapes(tiles, rows, latent):
    f32 = jnp.float32
    return [
        jax.ShapeDtypeStruct((tiles, rows, latent), f32),
        jax.ShapeDtypeStruct((tiles, rows, LANES), f32),
        jax.ShapeDtypeStruct((tiles, rows, LANES), f32),
    ]


def key_scratch(width, columns, rows, copies):
    scores = pltpu.VMEM((columns // SMALL, rows, SMALL), jnp.float32)
    window = pltpu.VMEM((width, columns), jnp.bfloat16)
    return window, scores, scores, pltpu.SemaphoreType.DMA((copies,))


def cost(queries, latent, columns):
    tiles, rows, width = queries.shape
    return pl.CostEstimate(
        flops=2 * tiles * rows * (width + latent) * columns,
        bytes_accessed=4 * MIB,
        transcendentals=tiles * rows * columns,
    )


def attend_own(factor, bounds, limits, queries, response, own_latent, own_rope):
    tiles, rows, width = queries.shape
    latent, block = own_latent.shape
    return pl.pallas_call(
        lambda *refs: own_kernel(factor, *refs),
        out_shape=state_shapes(tiles, rows, latent),
        in_specs=[SMEM] + [VMEM] * 3 + [ANYWHERE] * 2,
        out_specs=[VMEM] * 3,
        scratch_shapes=list(key_scratch(width, block, rows, 2)),
        name="attend_own",
        cost_estimate=cost(queries, latent, block),
        compiler_params=pltpu.CompilerParams(vmem_limit_bytes=16 * MIB),
    )(bounds, limits, queries, response, own_latent, own_rope)


def attend_near(factor, position, bounds, limits, queries, state, mine, theirs):
    tiles, rows, width = queries.shape
    latent = state[0].shape[2]
    block = mine[0].shape[1]
    return pl.pallas_call(
        lambda *refs: near_kernel(factor, *refs),
        out_shape=state_shapes(tiles, rows, latent),
        in_specs=[SMEM, SMEM] + [VMEM] * 5 + [ANYWHERE] * 4,
        out_specs=[VMEM] * 3,
        scratch_shapes=list(key_scratch(width, 4 * block, rows, 4)),
        input_output_aliases={4: 0},
        name="attend_near",
        cost_estimate=cost(queries, latent, 2 * block),
        compiler_params=pltpu.CompilerParams(vmem_limit_bytes=36 * MIB),
    )(position, bounds, limits, queries, *state, mine[0], theirs[0], mine[1], theirs[1])


def attend_far(factor, position, bounds, limits, queries, state, value, order, mine, theirs):
    head_count, latent, value_width = value.shape
    tiles, rows, width = queries.shape
    block = mine.shape[1]
    f32 = jnp.float32
    window, even, odd, sems = key_scratch(width, 2 * block, rows, 2)
    return pl.pallas_call(
        lambda *refs: far_kernel(factor, *refs),
        out_shape=jax.ShapeDtypeStruct(
            (tiles * TILE // GROUP, GROUP, head_count * value_width), jnp.bfloat16
        ),
        in_specs=[SMEM, SMEM] + [VMEM] * 7 + [ANYWHERE] * 2,
        out_specs=VMEM,
        scratch_shapes=[
            window,
            even,
            odd,
            pltpu.VMEM((tiles, rows, latent), f32),
            pltpu.VMEM((tiles, rows, LANES), f32),
            pltpu.VMEM((tiles, rows, LANES), f32),
            pltpu.VMEM((head_count, tiles * TILE, latent), jnp.bfloat16),
            pltpu.VMEM((tiles * TILE, head_count * value_width), jnp.bfloat16),
            sems,
        ],
        name="attend_far",
        cost_estimate=cost(queries, latent, block),
        compiler_params=pltpu.CompilerParams(vmem_limit_bytes=30 * MIB),
    )(position, bounds, limits, queries, *state, value, order, mine, theirs)


def local(
    query_nope,
    query_rope,
    absorb_key,
    value_absorption_matrix,
    prompt_latent,
    prompt_rope,
    response_latent,
    response_rope,
    prompt_lengths,
    prompt_of,
    response_start,
):
    head_count, nope_width, latent_width = absorb_key.shape
    value_width = value_absorption_matrix.shape[2]
    rope_width = prompt_rope.shape[0]
    block = prompt_latent.shape[1]
    tokens = response_latent.shape[1]
    groups = lax.axis_size("head")
    length = lax.axis_size("seq")
    seq_index = lax.axis_index("seq")
    head_index = lax.axis_index("head")
    per = tokens // groups
    factor = (nope_width + rope_width) ** (-0.5) * math.log2(math.e)

    sent, response = pack(query_nope, query_rope, response_latent, response_rope, groups)
    position = jnp.stack(
        [seq_index * tokens, head_index % 2, (seq_index - REACH) * block]
    ).astype(jnp.int32)
    def onward(distance):
        return [
            (i * groups + h, (i + by) * groups + h)
            for i in range(length)
            for h in range(groups)
            for by in (distance * (1 - 2 * (h % 2)),)
            if 0 <= i + by < length
        ]

    swapped = [(h, h ^ 1) for h in range(groups)]

    arrived = lax.all_to_all(sent, "head", split_axis=0, concat_axis=0, tiled=True)
    queries, limits, order, bounds = absorb(
        position,
        prompt_lengths,
        prompt_of,
        response_start,
        arrived.reshape(tokens, head_count * (nope_width + rope_width)),
        absorb_key,
        rope_width,
    )
    queries = queries.reshape(tokens // TILE, head_count * TILE, latent_width + rope_width)

    first = join(
        lax.ppermute(prompt_latent, ("seq", "head"), onward(1)),
        lax.ppermute(prompt_rope, ("seq", "head"), onward(1)),
    )
    second = lax.ppermute(first, ("seq", "head"), onward(1))
    state = attend_own(
        factor, bounds, limits, queries, response, prompt_latent, prompt_rope
    )
    second, state = lax.optimization_barrier((second, state))
    third = lax.ppermute(second, ("seq", "head"), onward(1))
    near = [first, second]
    swaps = [lax.ppermute(held, "head", swapped) for held in near]
    state = attend_near(factor, position, bounds, limits, queries, state, near, swaps)
    third, state = lax.optimization_barrier((third, state))
    attended = attend_far(
        factor,
        position,
        bounds,
        limits,
        queries,
        state,
        value_absorption_matrix,
        order,
        third,
        lax.ppermute(third, "head", swapped),
    )
    returned = lax.all_to_all(attended, "head", split_axis=0, concat_axis=0, tiled=True)
    return returned.transpose(1, 0, 2).reshape(per, groups * head_count * value_width)


def solution(mesh):
    return jax.shard_map(
        local,
        mesh=mesh,
        in_specs=(
            P(("seq", "head"), None),
            P(("seq", "head"), None),
            P("head", None, None),
            P("head", None, None),
            P(None, "seq"),
            P(None, "seq"),
            P(None, "seq"),
            P(None, "seq"),
            P(),
            P("seq"),
            P("seq"),
        ),
        out_specs=P(("seq", "head"), None),
        check_vma=False,
    )
```
